32 devices in a mesh: seq: 4 (over y, core), ctx: 8 (over z, x).
Axes of the slice: x: 2, y: 2, z: 4, core: 2. Of those that a mesh axis runs over, the one named last changes fastest.
Arguments:
- tokens: bfloat16 [4, 1024, 2048], P('seq', 'ctx'), may hold values from -6 to 6
- positions: int32 [4, 1024], P('seq', 'ctx'), may hold values from 0 to 1022, as said below
- cotangent: bfloat16 [4, 1024, 2048], P('seq', 'ctx'), may hold values from -6 to 6
- w_query: bfloat16 [2048, 2048], P(('seq', 'ctx')), may hold values from -0.125 to 0.125
- w_key: bfloat16 [2048, 1024], P(('seq', 'ctx')), may hold values from -0.125 to 0.125
- w_value: bfloat16 [2048, 1024], P(('seq', 'ctx')), may hold values from -0.125 to 0.125
- w_out: bfloat16 [2048, 2048], P(('seq', 'ctx')), may hold values from -0.5 to 0.5
- w_gate: bfloat16 [2048, 6144], P(('seq', 'ctx')), may hold values from -0.125 to 0.125
- w_up: bfloat16 [2048, 6144], P(('seq', 'ctx')), may hold values from -0.125 to 0.125
- w_down: bfloat16 [6144, 2048], P(('seq', 'ctx')), may hold values from -0.078125 to 0.078125
- attn_gain: bfloat16 [2048], P(('seq', 'ctx')), may hold values from 0.099609375 to 1.8984375
- mlp_gain: bfloat16 [2048], P(('seq', 'ctx')), may hold values from 0.099609375 to 1.8984375
- query_gain: bfloat16 [128], P(('seq', 'ctx')), may hold values from 1 to 2.5
- key_gain: bfloat16 [128], P(('seq', 'ctx')), may hold values from 1 to 2.5
Outputs:
- block_out: bfloat16 [4, 1024, 2048], P('seq', 'ctx')
- grad_tokens: float32 [4, 1024, 2048], P('seq', 'ctx')
- grad_query: float32 [2048, 2048], P(('seq', 'ctx'))
- grad_key: float32 [2048, 1024], P(('seq', 'ctx'))
- grad_value: float32 [2048, 1024], P(('seq', 'ctx'))
- grad_out: float32 [2048, 2048], P(('seq', 'ctx'))
- grad_gate: float32 [2048, 6144], P(('seq', 'ctx'))
- grad_up: float32 [2048, 6144], P(('seq', 'ctx'))
- grad_down: float32 [6144, 2048], P(('seq', 'ctx'))
- grad_attn_gain: float32 [2048], P(('seq', 'ctx'))
- grad_mlp_gain: float32 [2048], P(('seq', 'ctx'))
- grad_query_gain: float32 [128], P(('seq', 'ctx'))
- grad_key_gain: float32 [128], P(('seq', 'ctx'))
The draws below stay inside these ranges and needn't reach their ends.
Inputs may be any that keep to these rules, and one draw needn't show every extreme that they name: `positions`: each sequence is cut into contiguous documents, and a token's position is its index minus the index of its document's first token. In one sequence, drawn from the seed, the first document is one token long and the second fills the rest of the sequence. In every other sequence each document has from max(1, 50) to 500 tokens, drawn evenly, and only the last one may be cut shorter by the sequence's end.
All inputs are finite; a program needn't handle non-finite values.
Results may differ from the reference program's by a relative error of at most 0.017.
The reference program's roundings to bfloat16 on the way count: a program that leaves them out, or rounds other values in their place, can miss the bound.
Values may be sent and summed in bfloat16 or wider, within the bound.
No kernel may reach another device: no remote copies, remote signals or barrier semaphores. Data moves between devices by JAX's collectives and lax.ppermute only.
A program may use at most 512 MiB of HBM per device.

```python
import math
import jax
import jax.numpy as jnp
from jax import lax

D = 2048
HEADS = 16
KV_HEADS = 8
HEAD_DIM = 128
FF = 6144
SEQS = 4
LENGTH = 1024


def draw_positions(key, part):
    key = jax.random.fold_in(key, 7)
    size_key, pick_key = jax.random.split(key, 2)
    shortest = max(1, LENGTH * 200 // 4096)
    longest = max(shortest, LENGTH * 2000 // 4096)
    count = LENGTH // shortest + 2
    sizes = jax.random.randint(size_key, (SEQS, count), shortest, longest + 1).astype(jnp.int32)
    chosen = jax.random.randint(pick_key, (), 0, SEQS).astype(jnp.int32)
    rows = jnp.arange(SEQS, dtype=jnp.int32)[:, None]
    column = jnp.arange(count, dtype=jnp.int32)[None, :]
    special = jnp.where(column == 0, 1, jnp.where(column == 1, LENGTH - 1, LENGTH)).astype(jnp.int32)
    sizes = jnp.where(rows == chosen, special, sizes)
    ends = jnp.cumsum(sizes, axis=1).astype(jnp.int32)
    starts = (ends - sizes).astype(jnp.int32)
    index = jnp.arange(LENGTH, dtype=jnp.int32)
    begun = starts[:, None, :] <= index[None, :, None]
    start = jnp.max(jnp.where(begun, starts[:, None, :], 0), axis=-1).astype(jnp.int32)
    return (index[None, :] - start).astype(jnp.int32)


def block_scale(key, extent, cuts, smallest, top_value):
    def one(position, blocks):
        draws = jax.random.uniform(jax.random.fold_in(jax.random.fold_in(key, 6), position), (blocks,), jnp.float32, smallest / len(cuts), top_value / len(cuts))
        return jnp.repeat(jnp.exp(draws), extent[position] // blocks).reshape((-1,) + (1,) * (len(extent) - position - 1))

    factor_of = one(*cuts[0])
    for cut in cuts[1:]:
        factor_of = factor_of * one(*cut)
    return factor_of


def scatter_about(own_key, dims, width, reach, pieces=(), kind=jnp.bfloat16):
    entries = jax.random.normal(own_key, dims, jnp.float32) * width
    if len(pieces) > 0:
        entries = block_scale(own_key, dims, pieces, -0.22, 0.18) * entries
    return jnp.clip(entries, min=-reach, max=reach).astype(kind)


def setup_inputs(seed: int = 0) -> dict:
    seeds = jax.random.split(jax.random.key(seed), 15)
    return {
        "tokens": scatter_about(seeds[0], (SEQS, LENGTH, D), 1.0, 6.0, ((0, 4), (1, 8))),
        "positions": draw_positions(jax.random.fold_in(seeds[14], 71), 0),
        "cotangent": scatter_about(seeds[2], (SEQS, LENGTH, D), 1.0, 6.0, ((0, 4), (1, 8))),
        "w_query": scatter_about(seeds[3], (D, HEADS * HEAD_DIM), D ** -0.5, 0.125, ((0, 32),)),
        "w_key": scatter_about(seeds[4], (D, KV_HEADS * HEAD_DIM), D ** -0.5, 0.125, ((0, 32),)),
        "w_value": scatter_about(seeds[5], (D, KV_HEADS * HEAD_DIM), D ** -0.5, 0.125, ((0, 32),)),
        "w_out": scatter_about(seeds[6], (HEADS * HEAD_DIM, D), (HEADS * HEAD_DIM // 16) ** -0.5, 0.5, ((0, 32),)),
        "w_gate": scatter_about(seeds[7], (D, FF), D ** -0.5, 0.125, ((0, 32),)),
        "w_up": scatter_about(seeds[8], (D, FF), D ** -0.5, 0.125, ((0, 32),)),
        "w_down": scatter_about(seeds[9], (FF, D), FF ** -0.5, 0.078125, ((0, 32),)),
        "attn_gain": jnp.clip(1.0 + 0.18 * jax.random.normal(seeds[10], (D,), jnp.float32), 0.099609375, 1.8984375).astype(jnp.bfloat16),
        "mlp_gain": jnp.clip(1.0 + 0.18 * jax.random.normal(seeds[11], (D,), jnp.float32), 0.099609375, 1.8984375).astype(jnp.bfloat16),
        "query_gain": jnp.clip(jnp.exp(math.log(2.5) - 0.916290732 * jax.random.uniform(seeds[12], (HEAD_DIM,), jnp.float32) ** block_scale(seeds[12], (HEAD_DIM,), ((0, 32),), -0.2, 0.2)), 1.0, 2.5).astype(jnp.bfloat16),
        "key_gain": jnp.clip(jnp.exp(math.log(2.5) - 0.916290732 * jax.random.uniform(seeds[13], (HEAD_DIM,), jnp.float32) ** block_scale(seeds[13], (HEAD_DIM,), ((0, 32),), -0.2, 0.2)), 1.0, 2.5).astype(jnp.bfloat16),
    }


EPS = 1e-06
THETA = 1000000.0
NEG = -1e+30

@jax.custom_vjp
def low(v):
    return lax.optimization_barrier(v.astype(jnp.bfloat16)).astype(jnp.float32)

@jax.custom_vjp
def low_back(v):
    return v

def low_keep(v):
    return (low(v), None)

def low_pass(kept, grad):
    return (grad,)

def back_keep(v):
    return (v, None)

def back_low(kept, grad):
    return (low(grad),)
low.defvjp(low_keep, low_pass)
low_back.defvjp(back_keep, back_low)

def product(left, right):
    return jnp.dot(left, right, precision=lax.Precision.HIGHEST, preferred_element_type=jnp.float32)

def root_norm(value, gain):
    return value * lax.rsqrt(lax.optimization_barrier(jnp.mean(value * value, axis=-1, keepdims=True)) + EPS) * gain

def rotate(value, where):
    half = value.shape[-1] // 2
    freq = THETA ** (-jnp.arange(half, dtype=jnp.float32) * 2.0 / value.shape[-1])
    angle = where.astype(jnp.float32)[:, None] * freq[None, :]
    cosine = jnp.cos(angle)[:, None, :]
    sine = jnp.sin(angle)[:, None, :]
    first = value[..., :half]
    second = value[..., half:]
    return jnp.concatenate([first * cosine - second * sine, second * cosine + first * sine], axis=-1)

def attend(query, keys, values, where):
    length = query.shape[0]
    group = query.shape[1] // keys.shape[1]
    block = min(512, length)
    count = length // block
    scale = query.shape[-1] ** (-0.5)
    query_blocks = query.reshape(count, block, keys.shape[1], group, query.shape[-1])
    where_blocks = where.reshape(count, block)
    starts = jnp.arange(count, dtype=jnp.int32) * block
    spots = jnp.arange(length, dtype=jnp.int32)

    def one_block(items):
        query_part, where_part, start = items
        place = start + jnp.arange(block, dtype=jnp.int32)
        scores = jnp.einsum('tkgd,skd->kgts', query_part, keys, precision=lax.Precision.HIGHEST) * scale
        visible = (spots[None, :] <= place[:, None]) & (spots[None, :] >= (place - where_part)[:, None])
        scores = low_back(jnp.where(visible[None, None], scores, NEG))
        peak = lax.optimization_barrier(jnp.max(scores, axis=-1, keepdims=True))
        powers = jnp.exp(scores - peak)
        share = low(powers / lax.optimization_barrier(jnp.sum(powers, axis=-1, keepdims=True)))
        return jnp.einsum('kgts,skd->tkgd', share, values, precision=lax.Precision.HIGHEST)
    result = lax.map(jax.checkpoint(one_block), (query_blocks, where_blocks, starts))
    return result.reshape(length, query.shape[1] * query.shape[-1])

def layer(inputs, weights, where):
    wquery, wkey, wvalue, wout, wgate, wup, wdown, gain_attn, gain_mlp, gain_query, gain_key = weights
    length = inputs.shape[0]
    head_dim = gain_query.shape[0]
    normed_one = low(root_norm(inputs, gain_attn))
    query = low_back(product(normed_one, wquery)).reshape(length, -1, head_dim)
    keys = low_back(product(normed_one, wkey)).reshape(length, -1, head_dim)
    values = low(low_back(product(normed_one, wvalue))).reshape(length, -1, head_dim)
    query = low(rotate(root_norm(query, gain_query), where))
    keys = low(rotate(root_norm(keys, gain_key), where))
    heads_out = low(low_back(attend(query, keys, values, where)))
    resid = inputs + low_back(product(heads_out, wout))
    normed_two = low(root_norm(resid, gain_mlp))
    gate = low_back(product(normed_two, wgate))
    upval = low_back(product(normed_two, wup))
    hidden = low(jax.nn.silu(gate) * upval)
    return resid + product(hidden, wdown)

def reference(tokens, positions, cotangent, w_query, w_key, w_value, w_out, w_gate, w_up, w_down, attn_gain, mlp_gain, query_gain, key_gain):
    weights = tuple((item.astype(jnp.float32) for item in (w_query, w_key, w_value, w_out, w_gate, w_up, w_down, attn_gain, mlp_gain, query_gain, key_gain)))

    def per_sequence(totals, items):
        inputs, where, upstream = items
        result, pull = jax.vjp(lambda source, params: layer(source, params, where), inputs.astype(jnp.float32), weights)
        grad_inputs, grad_weights = pull(upstream.astype(jnp.float32))
        totals = jax.tree.map(lambda left, right: left + right, totals, grad_weights)
        return (totals, (result.astype(jnp.bfloat16), grad_inputs))
    zeros = tuple((jnp.zeros(item.shape, jnp.float32) for item in weights))
    totals, (outputs, grad_inputs) = lax.scan(per_sequence, zeros, (tokens, positions, cotangent))
    return (outputs, grad_inputs) + tuple(totals)
```

```python
from functools import partial

import jax
import jax.numpy as jnp
from jax import lax
from jax.experimental import pallas as pl
from jax.experimental.pallas import tpu as pltpu
from jax.sharding import PartitionSpec as P

HEADS = 16
KV_HEADS = 8
HEAD_DIM = 128


EPS = 1e-06
THETA = 1000000.0
NEG = -1e30


def root_norm(value, gain):
    return value * lax.rsqrt(jnp.mean(value * value, axis=-1, keepdims=True) + EPS) * gain


def rotate(value, where):
    half = value.shape[-1] // 2
    freq = THETA ** (-jnp.arange(half, dtype=jnp.float32) * 2.0 / value.shape[-1])
    angle = where.astype(jnp.float32)[:, None] * freq[None, :]
    cosine = jnp.cos(angle)[:, None, :]
    sine = jnp.sin(angle)[:, None, :]
    first = value[..., :half]
    second = value[..., half:]
    return jnp.concatenate(
        [first * cosine - second * sine, second * cosine + first * sine], axis=-1
    )


def head_prep(value, gain, where):
    return rotate(root_norm(value, gain), where)


def swiglu(gate, upval):
    return jax.nn.silu(gate) * upval


def product(left, right):
    return jnp.dot(left, right, preferred_element_type=jnp.float32)


def product_left(left, right):
    return lax.dot_general(
        left, right, (((0,), (0,)), ((), ())), preferred_element_type=jnp.float32
    )


def product_right(left, right):
    return lax.dot_general(
        left, right, (((1,), (1,)), ((), ())), preferred_element_type=jnp.float32
    )


def whole_body(
    tokens,
    positions,
    cotangent,
    w_query,
    w_key,
    w_value,
    w_out,
    w_gate,
    w_up,
    w_down,
    attn_gain,
    mlp_gain,
    query_gain,
    key_gain,
):
    rows = tokens.shape[1]
    group = HEADS // KV_HEADS
    scale = HEAD_DIM ** (-0.5)
    inputs = tokens[0].astype(jnp.float32)
    where = positions[0]
    upstream = cotangent[0]
    place = lax.axis_index("ctx") * rows + jnp.arange(rows, dtype=jnp.int32)
    full_query, full_key, full_value, full_out, gain_attn, gain_query, gain_key = (
        lax.all_gather(w_query, ("seq", "ctx"), axis=0, tiled=True),
        lax.all_gather(w_key, ("seq", "ctx"), axis=0, tiled=True),
        lax.all_gather(w_value, ("seq", "ctx"), axis=0, tiled=True),
        lax.all_gather(w_out, ("seq", "ctx"), axis=0, tiled=True),
        lax.all_gather(attn_gain, ("seq", "ctx"), axis=0, tiled=True),
        lax.all_gather(query_gain, ("seq", "ctx"), axis=0, tiled=True),
        lax.all_gather(key_gain, ("seq", "ctx"), axis=0, tiled=True),
    )
    normed_one, pull_one = jax.vjp(root_norm, inputs, gain_attn.astype(jnp.float32))
    low_one = normed_one.astype(jnp.bfloat16)
    query_raw = product(low_one, full_query).reshape(rows, HEADS, HEAD_DIM)
    key_raw = product(low_one, full_key).reshape(rows, KV_HEADS, HEAD_DIM)
    value_low = product(low_one, full_value).astype(jnp.bfloat16)
    prepare = partial(head_prep, where=where)
    query_rot, pull_query = jax.vjp(prepare, query_raw, gain_query.astype(jnp.float32))
    key_rot, pull_key = jax.vjp(prepare, key_raw, gain_key.astype(jnp.float32))
    query_low = query_rot.astype(jnp.bfloat16).reshape(rows, KV_HEADS, group, HEAD_DIM)
    key_low = key_rot.astype(jnp.bfloat16).reshape(rows, KV_HEADS * HEAD_DIM)
    keys_all, values_all = (
        lax.all_gather(key_low, "ctx", axis=0, tiled=True),
        lax.all_gather(value_low, "ctx", axis=0, tiled=True),
    )
    length = keys_all.shape[0]
    keys_three = keys_all.reshape(length, KV_HEADS, HEAD_DIM)
    values_three = values_all.reshape(length, KV_HEADS, HEAD_DIM)
    spots = jnp.arange(length, dtype=jnp.int32)
    visible = (spots[None, :] <= place[:, None]) & (spots[None, :] >= (place - where)[:, None])

    def score_block():
        raw = (
            jnp.einsum("tkgd,skd->kgts", query_low, keys_three, preferred_element_type=jnp.float32)
            * scale
        )
        return jnp.where(visible[None, None], raw, NEG)

    scores = score_block()
    peak = jnp.max(scores, axis=-1, keepdims=True)
    powers = jnp.exp(scores - peak)
    totals = jnp.sum(powers, axis=-1, keepdims=True)
    share = powers / totals
    log_total = peak + jnp.log(totals)
    heads_out = jnp.einsum(
        "kgts,skd->tkgd",
        share.astype(jnp.bfloat16),
        values_three,
        preferred_element_type=jnp.float32,
    )
    heads_low = heads_out.reshape(rows, HEADS * HEAD_DIM).astype(jnp.bfloat16)
    resid = inputs + product(heads_low, full_out)
    full_gate, full_up, full_down, gain_mlp = (
        lax.all_gather(w_gate, ("seq", "ctx"), axis=0, tiled=True),
        lax.all_gather(w_up, ("seq", "ctx"), axis=0, tiled=True),
        lax.all_gather(w_down, ("seq", "ctx"), axis=0, tiled=True),
        lax.all_gather(mlp_gain, ("seq", "ctx"), axis=0, tiled=True),
    )
    normed_two, pull_two = jax.vjp(root_norm, resid, gain_mlp.astype(jnp.float32))
    low_two = normed_two.astype(jnp.bfloat16)
    gate = product(low_two, full_gate)
    upval = product(low_two, full_up)
    hidden, pull_hidden = jax.vjp(swiglu, gate, upval)
    hidden_low = hidden.astype(jnp.bfloat16)
    block_out = (resid + product(hidden_low, full_down)).astype(jnp.bfloat16)
    back_gate, back_up, back_down = (
        lax.all_gather(w_gate, ("seq", "ctx"), axis=0, tiled=True),
        lax.all_gather(w_up, ("seq", "ctx"), axis=0, tiled=True),
        lax.all_gather(w_down, ("seq", "ctx"), axis=0, tiled=True),
    )
    grad_hidden = product_right(upstream, back_down)
    grad_down = lax.psum_scatter(
        product_left(hidden_low, upstream), ("seq", "ctx"), scatter_dimension=0, tiled=True
    )
    grad_gate_act, grad_up_act = pull_hidden(grad_hidden)
    gate_low = grad_gate_act.astype(jnp.bfloat16)
    up_low = grad_up_act.astype(jnp.bfloat16)
    grad_normed_two = product_right(gate_low, back_gate) + product_right(up_low, back_up)
    resid_part, grad_gain_mlp = pull_two(grad_normed_two)
    grad_resid = upstream.astype(jnp.float32) + resid_part
    grad_gate, grad_up, grad_mlp_gain = (
        lax.psum_scatter(
            product_left(low_two, gate_low), ("seq", "ctx"), scatter_dimension=0, tiled=True
        ),
        lax.psum_scatter(
            product_left(low_two, up_low), ("seq", "ctx"), scatter_dimension=0, tiled=True
        ),
        lax.psum_scatter(grad_gain_mlp, ("seq", "ctx"), scatter_dimension=0, tiled=True),
    )
    back_query, back_key, back_value, back_out = (
        lax.all_gather(w_query, ("seq", "ctx"), axis=0, tiled=True),
        lax.all_gather(w_key, ("seq", "ctx"), axis=0, tiled=True),
        lax.all_gather(w_value, ("seq", "ctx"), axis=0, tiled=True),
        lax.all_gather(w_out, ("seq", "ctx"), axis=0, tiled=True),
    )
    resid_low = grad_resid.astype(jnp.bfloat16)
    grad_out_part = product_left(heads_low, resid_low)
    grad_heads = (
        product_right(resid_low, back_out)
        .astype(jnp.bfloat16)
        .reshape(rows, KV_HEADS, group, HEAD_DIM)
    )
    share_again = jnp.exp(score_block() - log_total)
    grad_share = jnp.einsum(
        "tkgd,skd->kgts", grad_heads, values_three, preferred_element_type=jnp.float32
    )
    grad_values_all = jnp.einsum(
        "kgts,tkgd->skd",
        share_again.astype(jnp.bfloat16),
        grad_heads,
        preferred_element_type=jnp.float32,
    )
    balance = jnp.sum(share_again * grad_share, axis=-1, keepdims=True)
    grad_scores = (share_again * (grad_share - balance)).astype(jnp.bfloat16)
    grad_query_rot = (
        jnp.einsum("kgts,skd->tkgd", grad_scores, keys_three, preferred_element_type=jnp.float32)
        * scale
    )
    grad_keys_all = (
        jnp.einsum("kgts,tkgd->skd", grad_scores, query_low, preferred_element_type=jnp.float32)
        * scale
    )
    grad_keys, grad_values = (
        lax.psum_scatter(
            grad_keys_all.reshape(length, KV_HEADS * HEAD_DIM),
            "ctx",
            scatter_dimension=0,
            tiled=True,
        ),
        lax.psum_scatter(
            grad_values_all.reshape(length, KV_HEADS * HEAD_DIM),
            "ctx",
            scatter_dimension=0,
            tiled=True,
        ),
    )
    grad_query_raw, grad_gain_query = pull_query(grad_query_rot.reshape(rows, HEADS, HEAD_DIM))
    grad_key_raw, grad_gain_key = pull_key(grad_keys.reshape(rows, KV_HEADS, HEAD_DIM))
    query_back = grad_query_raw.reshape(rows, HEADS * HEAD_DIM).astype(jnp.bfloat16)
    key_back = grad_key_raw.reshape(rows, KV_HEADS * HEAD_DIM).astype(jnp.bfloat16)
    value_back = grad_values.astype(jnp.bfloat16)
    grad_normed_one = (
        product_right(query_back, back_query)
        + product_right(key_back, back_key)
        + product_right(value_back, back_value)
    )
    input_part, grad_gain_attn = pull_one(grad_normed_one)
    grad_tokens = grad_resid + input_part
    grad_query, grad_key, grad_value, grad_out, grad_attn_gain, grad_query_gain, grad_key_gain = (
        lax.psum_scatter(
            product_left(low_one, query_back), ("seq", "ctx"), scatter_dimension=0, tiled=True
        ),
        lax.psum_scatter(
            product_left(low_one, key_back), ("seq", "ctx"), scatter_dimension=0, tiled=True
        ),
        lax.psum_scatter(
            product_left(low_one, value_back), ("seq", "ctx"), scatter_dimension=0, tiled=True
        ),
        lax.psum_scatter(grad_out_part, ("seq", "ctx"), scatter_dimension=0, tiled=True),
        lax.psum_scatter(grad_gain_attn, ("seq", "ctx"), scatter_dimension=0, tiled=True),
        lax.psum_scatter(grad_gain_query, ("seq", "ctx"), scatter_dimension=0, tiled=True),
        lax.psum_scatter(grad_gain_key, ("seq", "ctx"), scatter_dimension=0, tiled=True),
    )
    return (
        block_out[None],
        grad_tokens[None],
        grad_query,
        grad_key,
        grad_value,
        grad_out,
        grad_gate,
        grad_up,
        grad_down,
        grad_attn_gain,
        grad_mlp_gain,
        grad_query_gain,
        grad_key_gain,
    )


def head_order(parts):
    half = parts // 2
    return [2 * (c % half) + c // half for c in range(parts)]


PAD = 16
DIGIT = 128


def fold_qkv_kernel(parts, query, key, value, gains, positions, out):
    own = query.shape[0]
    group = query.shape[1] // parts
    head = key.shape[1] // parts
    where = positions[...]
    high = (where >> 7).astype(jnp.float32).astype(jnp.bfloat16)
    rest = (where & (DIGIT - 1)).astype(jnp.float32).astype(jnp.bfloat16)
    rows = where.shape[1]
    count = gains.shape[1]
    for c, k in enumerate(head_order(parts)):
        out[c, :own, :group] = query[:, k * group : (k + 1) * group]
        out[c, :own, group : group + head] = key[:, k * head : (k + 1) * head]
        out[c, :own, group + head :] = value[:, k * head : (k + 1) * head]
        out[c, own:, :] = jnp.zeros((PAD, out.shape[2]), out.dtype)
        out[c, own : own + 1, :count] = gains[...]
        out[c, own + 1 : own + 2, :rows] = high
        out[c, own + 1 : own + 2, rows : 2 * rows] = rest


def fold_qkv(w_query, w_key, w_value, gains, positions, parts):
    own = w_query.shape[0]
    cols = (w_query.shape[1] + w_key.shape[1] + w_value.shape[1]) // parts
    return pl.pallas_call(
        partial(fold_qkv_kernel, parts),
        out_shape=jax.ShapeDtypeStruct((parts, own + PAD, cols), w_query.dtype),
        cost_estimate=pl.CostEstimate(flops=0, bytes_accessed=1200000, transcendentals=0),
    )(w_query, w_key, w_value, gains, positions)


def fold_ff_kernel(seqs, parts, gate, up, out):
    unit = gate.shape[1] // (seqs * parts)
    for c in range(parts):
        for s in range(seqs):
            at = (s * parts + c) * unit
            out[c, :, s * unit : (s + 1) * unit] = gate[:, at : at + unit]
            out[c, :, (seqs + s) * unit : (seqs + s + 1) * unit] = up[:, at : at + unit]


def fold_ff(w_gate, w_up, seqs, parts):
    own, hidden = w_gate.shape
    return pl.pallas_call(
        partial(fold_ff_kernel, seqs, parts),
        out_shape=jax.ShapeDtypeStruct((parts, own, 2 * hidden // parts), w_gate.dtype),
        cost_estimate=pl.CostEstimate(flops=0, bytes_accessed=3200000, transcendentals=0),
    )(w_gate, w_up)


def unfold_ff_kernel(seqs, parts, turned, gate, up):
    unit = gate.shape[1] // (seqs * parts)
    for c in range(parts):
        for s in range(seqs):
            at = (s * parts + c) * unit
            gate[:, at : at + unit] = turned[c, :, s * unit : (s + 1) * unit].astype(gate.dtype)
            up[:, at : at + unit] = turned[
                c, :, (seqs + s) * unit : (seqs + s + 1) * unit
            ].astype(up.dtype)


def unfold_ff(turned, seqs, parts):
    own = turned.shape[1]
    shape = jax.ShapeDtypeStruct((own, turned.shape[2] * parts // 2), jnp.float32)
    return pl.pallas_call(
        partial(unfold_ff_kernel, seqs, parts),
        out_shape=(shape, shape),
        cost_estimate=pl.CostEstimate(flops=0, bytes_accessed=5000000, transcendentals=0),
    )(turned)


def unfold_qkv_kernel(turned, query, key, value, gains):
    parts = turned.shape[0]
    own = query.shape[0]
    group = query.shape[1] // parts
    head = key.shape[1] // parts
    total = jnp.zeros((1, turned.shape[2]), jnp.float32)
    for c, k in enumerate(head_order(parts)):
        query[:, k * group : (k + 1) * group] = turned[c, :own, :group].astype(jnp.float32)
        key[:, k * head : (k + 1) * head] = turned[c, :own, group : group + head].astype(
            jnp.float32
        )
        value[:, k * head : (k + 1) * head] = turned[c, :own, group + head :].astype(jnp.float32)
        total = total + turned[c, own:, :].astype(jnp.float32)[:1]
    gains[...] = total


def unfold_qkv(turned, own):
    parts, _, cols = turned.shape
    group = cols * HEADS // (HEADS + 2 * KV_HEADS)
    head = (cols - group) // 2
    return pl.pallas_call(
        unfold_qkv_kernel,
        out_shape=(
            jax.ShapeDtypeStruct((own, parts * group), jnp.float32),
            jax.ShapeDtypeStruct((own, parts * head), jnp.float32),
            jax.ShapeDtypeStruct((own, parts * head), jnp.float32),
            jax.ShapeDtypeStruct((1, cols), jnp.float32),
        ),
        cost_estimate=pl.CostEstimate(flops=0, bytes_accessed=1900000, transcendentals=0),
    )(turned)


ROWS = 256


def turn_halves(value):
    return pltpu.roll(value, value.shape[1] // 2, 1)


def dot_right(left, right):
    return lax.dot_general(
        left, right, (((1,), (1,)), ((), ())), preferred_element_type=jnp.float32
    )


def dot_left(left, right):
    return lax.dot_general(
        left, right, (((0,), (0,)), ((), ())), preferred_element_type=jnp.float32
    )


def project_kernel(
    own, tokens, gathered, gain, cosine, sine, gain_query, gain_key,
    normed, raw, query, key, value, weight,
):
    head = gain_query.shape[1]
    group = query.shape[1] // head

    @pl.when(pl.program_id(0) == 0)
    def _():
        weight[...] = gathered[:, :own, :].reshape(weight.shape)

    x = tokens[...].astype(jnp.float32)
    low = root_norm(x, gain[...]).astype(jnp.bfloat16)
    normed[...] = low
    qkv = jnp.dot(low, weight[...], preferred_element_type=jnp.float32)
    raw[...] = qkv[:, : (group + 1) * head]
    value[...] = qkv[:, (group + 1) * head :].astype(jnp.bfloat16)
    cos = cosine[...]
    sin = sine[...]
    for h in range(group + 1):
        scale = gain_key[...] if h == group else gain_query[...]
        part = root_norm(qkv[:, h * head : (h + 1) * head], scale)
        part = (part * cos + turn_halves(part) * sin).astype(jnp.bfloat16)
        if h == group:
            key[...] = part
        else:
            query[:, h * head : (h + 1) * head] = part


def project(tokens, gathered, gain, cosine, sine, gain_query, gain_key, own):
    length, width = tokens.shape
    cols = gathered.shape[2]
    head = gain_query.shape[1]
    rows = min(ROWS, length)

    def block(n):
        return pl.BlockSpec((rows, n), lambda i: (i, 0))

    def whole(*shape):
        return pl.BlockSpec(shape, lambda i: (0,) * len(shape))

    def out(n, kind=jnp.bfloat16):
        return jax.ShapeDtypeStruct((length, n), kind)

    raw_cols = cols - head
    return pl.pallas_call(
        partial(project_kernel, own),
        grid=(length // rows,),
        in_specs=[
            block(width),
            whole(*gathered.shape),
            whole(1, width),
            block(head),
            block(head),
            whole(1, head),
            whole(1, head),
        ],
        out_specs=[
            block(width),
            block(raw_cols),
            block(raw_cols - head),
            block(head),
            block(head),
            whole(width, cols),
        ],
        out_shape=[
            out(width),
            out(raw_cols, jnp.float32),
            out(raw_cols - head),
            out(head),
            out(head),
            jax.ShapeDtypeStruct((width, cols), jnp.bfloat16),
        ],
        cost_estimate=pl.CostEstimate(
            flops=2 * length * width * cols, bytes_accessed=14000000, transcendentals=0
        ),
        compiler_params=pltpu.CompilerParams(vmem_limit_bytes=24 * 2**20),
    )(tokens, gathered, gain, cosine, sine, gain_query, gain_key)


def block_mask(start, first, rows, keys):
    spot = first + lax.broadcasted_iota(jnp.int32, (rows, keys), 0)
    other = lax.broadcasted_iota(jnp.int32, (rows, keys), 1)
    return (other <= spot) & (other >= start)


def attend_kernel(query, key, value, start, heads, lse):
    length = query.shape[0]
    head = key.shape[1]
    rows = min(ROWS, length)
    scale = head ** (-0.5)
    for i in range(length // rows):
        at = slice(i * rows, (i + 1) * rows)
        keys = (i + 1) * rows
        visible = block_mask(start[at, :], i * rows, rows, keys)
        for h in range(query.shape[1] // head):
            of = slice(h * head, (h + 1) * head)
            scores = dot_right(query[at, of], key[:keys, :]) * scale
            scores = jnp.where(visible, scores, NEG)
            peak = jnp.max(scores, axis=1, keepdims=True)
            powers = jnp.exp(scores - peak)
            total = jnp.sum(powers, axis=1, keepdims=True)
            share = (powers / total).astype(jnp.bfloat16)
            heads[at, of] = jnp.dot(
                share, value[:keys, :], preferred_element_type=jnp.float32
            ).astype(jnp.bfloat16)
            lse[at, h : h + 1] = peak + jnp.log(total)


def attend(query, key, value, start):
    length, cols = query.shape
    return pl.pallas_call(
        attend_kernel,
        out_shape=(
            jax.ShapeDtypeStruct((length, cols), jnp.bfloat16),
            jax.ShapeDtypeStruct((length, cols // key.shape[1]), jnp.float32),
        ),
        cost_estimate=pl.CostEstimate(
            flops=4 * length * length * cols, bytes_accessed=2600000, transcendentals=2 * length * length
        ),
        compiler_params=pltpu.CompilerParams(vmem_limit_bytes=24 * 2**20),
    )(query, key, value, start)


def norm_back(raw, gain, grad):
    r = lax.rsqrt(jnp.mean(raw * raw, axis=1, keepdims=True) + EPS)
    weighted = gain * grad
    back = r * weighted - (r * r * r) * raw * jnp.mean(weighted * raw, axis=1, keepdims=True)
    return back, jnp.sum(grad * raw * r, axis=0, keepdims=True)


def attend_back_kernel(
    query, key, value, start, lse, grads, raw, cosine, sine, gain_query, gain_key,
    back, part_query, part_key, grad_key, grad_value,
):
    length = query.shape[0]
    head = key.shape[1]
    group = query.shape[1] // head
    rows = min(ROWS, length)
    scale = head ** (-0.5)
    low = jnp.bfloat16
    grad_key[...] = jnp.zeros_like(grad_key)
    grad_value[...] = jnp.zeros_like(grad_value)
    total_query = jnp.zeros((1, head), jnp.float32)
    total_key = jnp.zeros((1, head), jnp.float32)
    for i in range(length // rows):
        at = slice(i * rows, (i + 1) * rows)
        keys = (i + 1) * rows
        visible = block_mask(start[at, :], i * rows, rows, keys)
        cos = cosine[at, :]
        sin = sine[at, :]
        for h in range(group):
            of = slice(h * head, (h + 1) * head)
            one = query[at, of]
            grad = grads[at, of]
            scores = jnp.where(visible, dot_right(one, key[:keys, :]) * scale, NEG)
            share = jnp.exp(scores - lse[at, h : h + 1])
            grad_share = dot_right(grad, value[:keys, :])
            grad_value[:keys, :] += dot_left(share.astype(low), grad)
            balance = jnp.sum(share * grad_share, axis=1, keepdims=True)
            grad_scores = (share * (grad_share - balance)).astype(low)
            turned = (
                jnp.dot(grad_scores, key[:keys, :], preferred_element_type=jnp.float32) * scale
            )
            grad_key[:keys, :] += dot_left(grad_scores, one)
            turned = turned * cos - turn_halves(turned) * sin
            result, term = norm_back(raw[at, of], gain_query[...], turned)
            back[at, of] = result.astype(low)
            total_query += term
    of = slice(group * head, (group + 1) * head)
    for i in range(length // rows):
        at = slice(i * rows, (i + 1) * rows)
        turned = grad_key[at, :] * scale
        turned = turned * cosine[at, :] - turn_halves(turned) * sine[at, :]
        result, term = norm_back(raw[at, of], gain_key[...], turned)
        back[at, of] = result.astype(low)
        total_key += term
        back[at, (group + 1) * head :] = grad_value[at, :].astype(low)
    part_query[...] = total_query
    part_key[...] = total_key


def attend_back(query, key, value, start, lse, grads, raw, cosine, sine, gain_query, gain_key):
    length, cols = query.shape
    head = key.shape[1]
    row = jax.ShapeDtypeStruct((1, head), jnp.float32)
    return pl.pallas_call(
        attend_back_kernel,
        out_shape=(
            jax.ShapeDtypeStruct((length, cols + 2 * head), jnp.bfloat16),
            row,
            row,
        ),
        scratch_shapes=[
            pltpu.VMEM((length, head), jnp.float32),
            pltpu.VMEM((length, head), jnp.float32),
        ],
        cost_estimate=pl.CostEstimate(
            flops=10 * length * length * cols, bytes_accessed=6000000, transcendentals=2 * length * length
        ),
        compiler_params=pltpu.CompilerParams(vmem_limit_bytes=28 * 2**20),
    )(query, key, value, start, lse, grads, raw, cosine, sine, gain_query, gain_key)


def pack_grads_kernel(own, normed, back, attn, mlp, query, key, out):
    owners = out.shape[0]
    small = query.shape[1] // owners
    low = out.dtype
    cols = out.shape[2]
    chunk = min(owners, 4)
    for first in range(0, owners, chunk):
        part = dot_left(normed[:, first * own : (first + chunk) * own], back[...]).astype(low)
        out[first : first + chunk, :own, :] = part.reshape(chunk, own, cols)
    out[:, own:, :] = jnp.zeros((owners, PAD, cols), low)
    for o in range(owners):
        row = slice(own, own + 1)
        out[o, row, :own] = attn[:, o * own : (o + 1) * own].astype(low)
        out[o, row, own : 2 * own] = mlp[:, o * own : (o + 1) * own].astype(low)
        out[o, row, 2 * own : 2 * own + small] = query[:, o * small : (o + 1) * small].astype(low)
        out[o, row, 2 * own + small : 2 * (own + small)] = key[
            :, o * small : (o + 1) * small
        ].astype(low)


def pack_grads(normed, back, attn, mlp, query, key, own):
    length, width = normed.shape
    cols = back.shape[1]
    owners = width // own
    return pl.pallas_call(
        partial(pack_grads_kernel, own),
        out_shape=jax.ShapeDtypeStruct((owners, own + PAD, cols), jnp.bfloat16),
        cost_estimate=pl.CostEstimate(
            flops=2 * length * width * cols, bytes_accessed=8000000, transcendentals=0
        ),
        compiler_params=pltpu.CompilerParams(vmem_limit_bytes=24 * 2**20),
    )(normed, back, attn, mlp, query, key).reshape(-1, cols)


def feed_kernel(count, *refs):
    arrived = refs[:count]
    upstream = refs[count : 2 * count]
    w_gu, w_down, hidden_out, gate_out, up_out, part_out, part_two = refs[2 * count :]
    low = jnp.bfloat16
    wide = w_down.shape[0]

    def join(pieces):
        return jnp.concatenate([piece[...] for piece in pieces], axis=0)

    normed = join(arrived)
    gate = jnp.dot(normed, w_gu[:, :wide], preferred_element_type=jnp.float32)
    up = jnp.dot(normed, w_gu[:, wide:], preferred_element_type=jnp.float32)
    grad_hidden = dot_right(join(upstream), w_down[...])
    s = jax.nn.sigmoid(gate)
    silu = gate * s
    hidden = (silu * up).astype(low)
    grad_gate = (grad_hidden * up * s * (1.0 + gate * (1.0 - s))).astype(low)
    grad_up = (grad_hidden * silu).astype(low)
    hidden_out[...] = hidden
    gate_out[...] = grad_gate
    up_out[...] = grad_up
    part_out[...] = jnp.dot(hidden, w_down[...], preferred_element_type=jnp.float32).astype(low)
    part_two[...] = (
        dot_right(grad_gate, w_gu[:, :wide]) + dot_right(grad_up, w_gu[:, wide:])
    ).astype(low)


def feed(arrived, upstream, w_gu, w_down):
    count = len(arrived)
    wide, width = w_down.shape
    rows = sum(item.shape[0] for item in arrived)
    low = jnp.bfloat16
    return pl.pallas_call(
        partial(feed_kernel, count),
        out_shape=[jax.ShapeDtypeStruct((rows, wide), low)] * 3
        + [jax.ShapeDtypeStruct((rows, width), low)] * 2,
        cost_estimate=pl.CostEstimate(
            flops=12 * rows * width * wide,
            bytes_accessed=6 * width * wide + 12 * rows * width,
            transcendentals=rows * wide,
        ),
        compiler_params=pltpu.CompilerParams(vmem_limit_bytes=22 * 2**20),
    )(*arrived, *upstream, w_gu, w_down)


def outer_kernel(counts, rights, *refs):
    out = refs[-1]
    at = 0
    lefts = []
    for count in counts:
        lefts.append(jnp.concatenate([item[...] for item in refs[at : at + count]], axis=0))
        at += count
    first = 0
    for sizes in rights:
        total = None
        for left, size in zip(lefts, sizes):
            right = jnp.concatenate([item[...] for item in refs[at : at + size]], axis=0)
            at += size
            term = dot_left(left, right)
            total = term if total is None else total + term
        out[:, first : first + total.shape[1]] = total.astype(out.dtype)
        first += total.shape[1]


def outer_sum(lefts, rights, tile):
    flat_left = [item for group in lefts for item in group]
    flat_right = [item for side in rights for group in side for item in group]
    tall = flat_left[0].shape[1]
    cols = sum(side[0][0].shape[1] for side in rights)
    length = sum(item.shape[0] for item in flat_left)
    return pl.pallas_call(
        partial(
            outer_kernel,
            [len(group) for group in lefts],
            [[len(group) for group in side] for side in rights],
        ),
        grid=(tall // tile,),
        in_specs=[pl.BlockSpec((item.shape[0], tile), lambda i: (0, i)) for item in flat_left]
        + [pl.BlockSpec(item.shape, lambda i: (0, 0)) for item in flat_right],
        out_specs=pl.BlockSpec((tile, cols), lambda i: (i, 0)),
        out_shape=jax.ShapeDtypeStruct((tall, cols), jnp.bfloat16),
        cost_estimate=pl.CostEstimate(
            flops=2 * tall * cols * length,
            bytes_accessed=2 * (tall * cols + length * (tall + cols)),
            transcendentals=0,
        ),
        compiler_params=pltpu.CompilerParams(vmem_limit_bytes=18 * 2**20),
    )(*flat_left, *flat_right)


def angles(where, head):
    half = head // 2
    freq = THETA ** (-jnp.arange(half, dtype=jnp.float32) * 2.0 / head)
    angle = where.astype(jnp.float32)[:, None] * freq[None, :]
    cosine = jnp.cos(angle)
    sine = jnp.sin(angle)
    return jnp.concatenate([cosine, cosine], axis=-1), jnp.concatenate([-sine, sine], axis=-1)


def grouped_body(
    seqs,
    parts,
    tokens,
    positions,
    cotangent,
    w_query,
    w_key,
    w_value,
    w_out,
    w_gate,
    w_up,
    w_down,
    attn_gain,
    mlp_gain,
    query_gain,
    key_gain,
):
    rows = tokens.shape[1]
    own = w_query.shape[0]
    group = HEADS // KV_HEADS
    length = rows * parts
    low = jnp.bfloat16
    unit = w_gate.shape[1] // (seqs * parts)
    wide = seqs * unit
    reach = parts // 2
    part = lax.axis_index("ctx")
    here = lax.axis_index("seq")
    small = query_gain.shape[0]

    ring = list(range(0, parts, 2)) + list(range(parts - 1, 0, -2))
    onward = [(ring[k], ring[(k + 1) % parts]) for k in range(parts)]
    backward = [(b, a) for a, b in onward]

    def right(value):
        return lax.ppermute(value, "ctx", onward)

    def left(value):
        return lax.ppermute(value, "ctx", backward)

    spot = jnp.where(part & 1 == 0, part >> 1, parts - ((part + 1) >> 1))
    begin = {}
    for step in range(1 - reach, reach + 1):
        ahead = (spot + (parts + step)) & (parts - 1)
        begin[step] = jnp.where(ahead < reach, 2 * ahead, 2 * (parts - ahead) - 1) * rows

    def hold(values, others):
        return lax.optimization_barrier((values, others))[0]

    done = {}

    def step_out(sent, jobs):
        sent = hold(sent, ())
        got = [(right(ahead), left(behind)) for ahead, behind in sent]
        job = jobs.pop(0) if jobs else None
        got, made = hold((got, () if job is None else job(sent)), ())
        if isinstance(made, dict):
            done.update(made)
        return got

    def ring_pieces(value, jobs=()):
        jobs = list(jobs)
        half = rows // 2
        pieces = [(value,)]
        ahead = behind = value
        for step in range(1, reach + 1):
            if step == reach:
                ahead, behind = ahead[:half], behind[half:]
            if jobs and jobs[0] is not None:
                jobs[0] = partial(jobs[0], pieces[-1])
            ((ahead, behind),) = step_out([(ahead, behind)], jobs)
            pieces.append((ahead, behind))
        return pieces

    def ring_gather(value, base, jobs=()):
        def drop(job):
            return None if job is None else lambda piece, sent: job(sent)

        pieces = ring_pieces(value, [drop(job) for job in jobs])
        done["last"] = pieces[-1]
        return whole_of(pieces, base)

    def whole_of(pieces, base):
        put = partial(lax.dynamic_update_slice_in_dim, axis=0, allow_negative_indices=False)
        whole = put(base, pieces[0][0], begin[0])
        for step in range(1, reach):
            whole = put(put(whole, pieces[step][0], begin[-step]), pieces[step][1], begin[step])
        whole = put(whole, pieces[reach][0], begin[reach])
        return put(whole, pieces[reach][1], begin[reach] + rows // 2)

    def ring_scatter(rings, jobs=()):
        jobs = list(jobs)
        half = rows // 2
        wider = jnp.float32

        def widen(pair):
            return pair[0].astype(wider), pair[1].astype(wider)

        got = step_out([(terms[reach][:half], terms[reach][half:]) for terms in rings], jobs)
        got = [
            (jnp.pad(ahead, ((0, half), (0, 0))), jnp.pad(behind, ((half, 0), (0, 0))))
            for ahead, behind in map(widen, got)
        ]
        for step in range(reach - 1, 0, -1):
            sent = [
                (
                    (terms[step][rows:].astype(wider) + ahead).astype(low),
                    (terms[step][:rows].astype(wider) + behind).astype(low),
                )
                for terms, (ahead, behind) in zip(rings, got)
            ]
            got = [widen(pair) for pair in step_out(sent, jobs)]
        return [
            terms[0].astype(wider) + ahead + behind for terms, (ahead, behind) in zip(rings, got)
        ]

    def ring_terms(value):
        def cut(step):
            return lax.dynamic_slice_in_dim(
                value, begin[step], rows, 0, allow_negative_indices=False
            ).astype(low)

        pairs = [jnp.concatenate([cut(-step), cut(step)]) for step in range(1, reach)]
        return [cut(0)] + pairs + [cut(reach)]

    def seq_gather(value):
        return lax.all_gather(value, "seq", axis=0, tiled=True)

    def seq_scatter(value):
        return lax.psum_scatter(value.astype(low), "seq", scatter_dimension=0, tiled=True)

    def cross(value, bit):
        return lax.ppermute(value, "seq", [(s, s ^ bit) for s in range(seqs)])

    def seq_scatter_near(value):
        size = value.shape[0] // seqs

        def cut(bits):
            return lax.dynamic_slice_in_dim(
                value, (here ^ bits) * size, size, 0, allow_negative_indices=False
            ).astype(low)

        far = cross(cut(3), 1).astype(jnp.float32)
        near = cross(cut(1), 1).astype(jnp.float32)
        other = cross((cut(2) + far).astype(low), 2).astype(jnp.float32)
        return cut(0) + near + other

    def turn(value):
        return lax.all_to_all(value, "ctx", split_axis=0, concat_axis=0, tiled=True)

    def swap_rows(value, back=False):
        pairs = [
            (a, (a % seqs) * parts + head_order(parts).index(a // seqs))
            for a in range(seqs * parts)
        ]
        if back:
            pairs = [(b, a) for a, b in pairs]
        return lax.ppermute(value, ("seq", "ctx"), pairs)

    my_x = tokens[0].astype(jnp.float32)
    upstream = cotangent[0]
    wide_q = group * HEAD_DIM
    wide_qkv = wide_q + 2 * HEAD_DIM
    tall = own + PAD
    packed = fold_qkv(
        w_query,
        w_key,
        w_value,
        jnp.concatenate([attn_gain, mlp_gain, query_gain, key_gain])[None],
        positions,
        parts,
    )

    def pack_first(sent):
        return packed

    def pack_second(sent):
        done["turned"] = turn(hold(packed, sent))
        done["folded"] = fold_ff(*hold((w_gate, w_up), sent), seqs, parts)
        return done["folded"]

    def pack_third(sent):
        done["turned"] = hold(done["turned"], sent)
        return ()

    def angle_part(sent):
        digits = done["turned"][:, own + 1, : 2 * rows].astype(jnp.float32)
        where = digits[:, :rows] * DIGIT + digits[:, rows:]
        done["where"] = hold(where.astype(jnp.int32).reshape(-1), sent)
        done["angles"] = angles(done["where"], HEAD_DIM)
        return done["angles"]

    full_x = ring_gather(
        tokens[0],
        jnp.zeros((length, tokens.shape[2]), low),
        [pack_first, pack_second, pack_third, angle_part],
    )
    turned = done["turned"]
    gathered = seq_gather(turned.reshape(parts * tall, wide_qkv)).reshape(-1, tall, wide_qkv)
    gains = gathered[:, own, : 2 * (own + small)].astype(jnp.float32)
    gain_attn = gains[:, :own].reshape(-1)
    gain_mlp = gains[:, own : 2 * own].reshape(-1)
    gain_query = gains[:, 2 * own : 2 * own + small].reshape(1, -1)
    gain_key = gains[:, 2 * own + small :].reshape(1, -1)
    start = (jnp.arange(length, dtype=jnp.int32) - done["where"])[:, None]
    cosine, sine = done["angles"]

    turned_gu = turn(hold(done["folded"], done["last"])).reshape(own * parts, -1)
    w_d = seq_gather(w_down)

    def first_part(sent):
        full, _ = hold((full_x, gathered), sent)
        done["first"] = project(
            full, gathered, gain_attn[None], cosine, sine, gain_query, gain_key, own
        )
        done["swapped"] = swap_rows(hold(w_out, sent))
        return done["first"], done["swapped"]

    def second_part(sent):
        _, _, query, key, value, _ = hold(done["first"], sent)
        done["w_out"] = seq_gather(hold(done["swapped"], sent))
        done["second"] = attend(query, key, value, start)
        return done["second"]

    def drop(job):
        return lambda piece, sent: job(sent)

    pieces_c = ring_pieces(hold(upstream, done["last"]), [drop(first_part), drop(second_part)])
    low_one, raw, query_low, key_low, value_low, w_qkv = done["first"]
    heads_low, lse = done["second"]
    w_o = done["w_out"]
    turned_gu, heads_low = hold((turned_gu, heads_low), (pieces_c[reach], w_d))
    w_gu = seq_gather(turned_gu)
    (summed,) = ring_scatter([ring_terms(product(hold(heads_low, turned_gu), w_o))])
    resid = my_x + summed

    normed_two, pull_two = jax.vjp(root_norm, resid, gain_mlp)
    fed = []

    def feed_next(piece, sent=()):
        fed.append(feed(hold(piece, sent), pieces_c[len(fed)], w_gu, w_d))
        return fed[-1]

    pieces_two = ring_pieces(normed_two.astype(low), [feed_next] * reach)
    feed_next(pieces_two[reach])
    hidden, grad_gate_act, grad_up_act, part_out, part_two = zip(*fed)

    def singly(items):
        return [(item,) for item in items]

    def sum_gu(sent):
        return {
            "gu": outer_sum(
                hold(pieces_two, sent), [singly(grad_gate_act), singly(grad_up_act)], 256
            )
        }

    def sum_down(sent):
        done["down"] = outer_sum(singly(hold(hidden, sent)), [pieces_c], 256)
        return done["down"]

    grad_normed_two, summed = ring_scatter([part_two, part_out], [sum_down, sum_gu])
    done["gu"] = seq_scatter(done["gu"])
    resid_part, part_mlp = pull_two(grad_normed_two)
    block_out = (resid + summed).astype(low)
    grad_resid = upstream.astype(jnp.float32) + resid_part
    heads_back = []

    def back_heads(piece, sent):
        heads_back.append(
            [product_right(item, w_o).astype(low) for item in hold(piece, sent)]
        )
        return heads_back[-1]

    def spread_down(piece, sent):
        done["down"] = seq_scatter_near(hold(done["down"], sent))
        return back_heads(piece, sent)

    def end_down(piece, sent):
        done["sent"] = sent
        return back_heads(piece, sent), done["down"]

    pieces_resid = ring_pieces(
        grad_resid.astype(low), [spread_down, back_heads, back_heads, end_down]
    )
    turned_grad = turn(hold(done["gu"], done["sent"]).reshape(parts, own, 2 * wide))
    back_heads(pieces_resid[reach], ())
    grad_heads = whole_of(heads_back, jnp.zeros((length, wide_q), low))
    done["back"] = attend_back(
        query_low,
        key_low,
        value_low,
        start,
        lse,
        grad_heads,
        raw,
        cosine,
        sine,
        gain_query,
        gain_key,
    )
    qkv_back, part_query, part_key = done["back"]
    part_normed_one = product_right(qkv_back, w_qkv)
    _, pull_gain = jax.vjp(
        lambda gain: root_norm(full_x.astype(jnp.float32), gain), gain_attn
    )

    def sum_qkv(sent):
        held = hold(qkv_back, sent)
        done["qkv"] = pack_grads(
            low_one,
            held,
            pull_gain(part_normed_one)[0][None],
            part_mlp[None],
            part_query,
            part_key,
            own,
        )
        pieces = [
            [lax.dynamic_slice_in_dim(heads_low, begin[0], rows, 0, allow_negative_indices=False)]
        ]
        half = rows // 2
        for step in range(1, reach + 1):
            size = rows if step < reach else half
            pieces.append(
                [
                    lax.dynamic_slice_in_dim(
                        heads_low, at, size, 0, allow_negative_indices=False
                    )
                    for at in (
                        (begin[-step], begin[step])
                        if step < reach
                        else (begin[reach], begin[reach] + half)
                    )
                ]
            )
        done["out"] = outer_sum(pieces, [hold(pieces_resid, sent)], wide_q)
        done["turned"] = hold(turned_grad, sent)
        return done["qkv"], done["out"], done["turned"]

    def end_gu(sent):
        done["gu"] = unfold_ff(hold(done["turned"], sent), seqs, parts)
        return done["gu"]

    (grad_normed_one,) = ring_scatter([ring_terms(part_normed_one)], [sum_qkv, end_gu])
    grad_gate, grad_up = done["gu"]
    grad_down = done["down"]
    summed = seq_scatter_near(done["qkv"]).astype(low)
    grad_query, grad_key, grad_value, gain_sums = unfold_qkv(
        turn(summed.reshape(parts, tall, wide_qkv)), own
    )
    gain_sums = gain_sums[0]
    grad_out = swap_rows(seq_scatter(done["out"]), back=True).astype(jnp.float32)
    _, pull_mine = jax.vjp(lambda value: root_norm(value, gain_attn), my_x)
    grad_tokens = grad_resid + pull_mine(grad_normed_one)[0]
    return (
        block_out[None],
        grad_tokens[None],
        grad_query,
        grad_key,
        grad_value,
        grad_out,
        grad_gate,
        grad_up,
        grad_down,
        gain_sums[:own],
        gain_sums[own : 2 * own],
        gain_sums[2 * own : 2 * own + small],
        gain_sums[2 * own + small : 2 * (own + small)],
    )


def solution(mesh):
    grouped = mesh.shape["ctx"] == KV_HEADS and mesh.shape["seq"] == 4
    return jax.shard_map(
        partial(grouped_body, mesh.shape["seq"], mesh.shape["ctx"]) if grouped else whole_body,
        mesh=mesh,
        in_specs=(
            P("seq", "ctx", None),
            P("seq", "ctx"),
            P("seq", "ctx", None),
            P(("seq", "ctx"), None),
            P(("seq", "ctx"), None),
            P(("seq", "ctx"), None),
            P(("seq", "ctx"), None),
            P(("seq", "ctx"), None),
            P(("seq", "ctx"), None),
            P(("seq", "ctx"), None),
            P(("seq", "ctx")),
            P(("seq", "ctx")),
            P(("seq", "ctx")),
            P(("seq", "ctx")),
        ),
        out_specs=(
            P("seq", "ctx", None),
            P("seq", "ctx", None),
            P(("seq", "ctx"), None),
            P(("seq", "ctx"), None),
            P(("seq", "ctx"), None),
            P(("seq", "ctx"), None),
            P(("seq", "ctx"), None),
            P(("seq", "ctx"), None),
            P(("seq", "ctx"), None),
            P(("seq", "ctx")),
            P(("seq", "ctx")),
            P(("seq", "ctx")),
            P(("seq", "ctx")),
        ),
        check_vma=False,
    )
```

```python
from functools import partial

import jax
import jax.numpy as jnp
from jax import lax
from jax.experimental import pallas as pl
from jax.experimental.pallas import tpu as pltpu
from jax.sharding import PartitionSpec as P

HEADS = 16
KV_HEADS = 8
HEAD_DIM = 128


EPS = 1e-06
THETA = 1000000.0
NEG = -1e30


def root_norm(value, gain):
    return value * lax.rsqrt(jnp.mean(value * value, axis=-1, keepdims=True) + EPS) * gain


def rotate(value, where):
    half = value.shape[-1] // 2
    freq = THETA ** (-jnp.arange(half, dtype=jnp.float32) * 2.0 / value.shape[-1])
    angle = where.astype(jnp.float32)[:, None] * freq[None, :]
    cosine = jnp.cos(angle)[:, None, :]
    sine = jnp.sin(angle)[:, None, :]
    first = value[..., :half]
    second = value[..., half:]
    return jnp.concatenate(
        [first * cosine - second * sine, second * cosine + first * sine], axis=-1
    )


def head_prep(value, gain, where):
    return rotate(root_norm(value, gain), where)


def swiglu(gate, upval):
    return jax.nn.silu(gate) * upval


def product(left, right):
    return jnp.dot(left, right, preferred_element_type=jnp.float32)


def product_left(left, right):
    return lax.dot_general(
        left, right, (((0,), (0,)), ((), ())), preferred_element_type=jnp.float32
    )


def product_right(left, right):
    return lax.dot_general(
        left, right, (((1,), (1,)), ((), ())), preferred_element_type=jnp.float32
    )


def whole_body(
    tokens,
    positions,
    cotangent,
    w_query,
    w_key,
    w_value,
    w_out,
    w_gate,
    w_up,
    w_down,
    attn_gain,
    mlp_gain,
    query_gain,
    key_gain,
):
    rows = tokens.shape[1]
    group = HEADS // KV_HEADS
    scale = HEAD_DIM ** (-0.5)
    inputs = tokens[0].astype(jnp.float32)
    where = positions[0]
    upstream = cotangent[0]
    place = lax.axis_index("ctx") * rows + jnp.arange(rows, dtype=jnp.int32)
    full_query, full_key, full_value, full_out, gain_attn, gain_query, gain_key = (
        lax.all_gather(w_query, ("seq", "ctx"), axis=0, tiled=True),
        lax.all_gather(w_key, ("seq", "ctx"), axis=0, tiled=True),
        lax.all_gather(w_value, ("seq", "ctx"), axis=0, tiled=True),
        lax.all_gather(w_out, ("seq", "ctx"), axis=0, tiled=True),
        lax.all_gather(attn_gain, ("seq", "ctx"), axis=0, tiled=True),
        lax.all_gather(query_gain, ("seq", "ctx"), axis=0, tiled=True),
        lax.all_gather(key_gain, ("seq", "ctx"), axis=0, tiled=True),
    )
    normed_one, pull_one = jax.vjp(root_norm, inputs, gain_attn.astype(jnp.float32))
    low_one = normed_one.astype(jnp.bfloat16)
    query_raw = product(low_one, full_query).reshape(rows, HEADS, HEAD_DIM)
    key_raw = product(low_one, full_key).reshape(rows, KV_HEADS, HEAD_DIM)
    value_low = product(low_one, full_value).astype(jnp.bfloat16)
    prepare = partial(head_prep, where=where)
    query_rot, pull_query = jax.vjp(prepare, query_raw, gain_query.astype(jnp.float32))
    key_rot, pull_key = jax.vjp(prepare, key_raw, gain_key.astype(jnp.float32))
    query_low = query_rot.astype(jnp.bfloat16).reshape(rows, KV_HEADS, group, HEAD_DIM)
    key_low = key_rot.astype(jnp.bfloat16).reshape(rows, KV_HEADS * HEAD_DIM)
    keys_all, values_all = (
        lax.all_gather(key_low, "ctx", axis=0, tiled=True),
        lax.all_gather(value_low, "ctx", axis=0, tiled=True),
    )
    length = keys_all.shape[0]
    keys_three = keys_all.reshape(length, KV_HEADS, HEAD_DIM)
    values_three = values_all.reshape(length, KV_HEADS, HEAD_DIM)
    spots = jnp.arange(length, dtype=jnp.int32)
    visible = (spots[None, :] <= place[:, None]) & (spots[None, :] >= (place - where)[:, None])

    def score_block():
        raw = (
            jnp.einsum("tkgd,skd->kgts", query_low, keys_three, preferred_element_type=jnp.float32)
            * scale
        )
        return jnp.where(visible[None, None], raw, NEG)

    scores = score_block()
    peak = jnp.max(scores, axis=-1, keepdims=True)
    powers = jnp.exp(scores - peak)
    totals = jnp.sum(powers, axis=-1, keepdims=True)
    share = powers / totals
    log_total = peak + jnp.log(totals)
    heads_out = jnp.einsum(
        "kgts,skd->tkgd",
        share.astype(jnp.bfloat16),
        values_three,
        preferred_element_type=jnp.float32,
    )
    heads_low = heads_out.reshape(rows, HEADS * HEAD_DIM).astype(jnp.bfloat16)
    resid = inputs + product(heads_low, full_out)
    full_gate, full_up, full_down, gain_mlp = (
        lax.all_gather(w_gate, ("seq", "ctx"), axis=0, tiled=True),
        lax.all_gather(w_up, ("seq", "ctx"), axis=0, tiled=True),
        lax.all_gather(w_down, ("seq", "ctx"), axis=0, tiled=True),
        lax.all_gather(mlp_gain, ("seq", "ctx"), axis=0, tiled=True),
    )
    normed_two, pull_two = jax.vjp(root_norm, resid, gain_mlp.astype(jnp.float32))
    low_two = normed_two.astype(jnp.bfloat16)
    gate = product(low_two, full_gate)
    upval = product(low_two, full_up)
    hidden, pull_hidden = jax.vjp(swiglu, gate, upval)
    hidden_low = hidden.astype(jnp.bfloat16)
    block_out = (resid + product(hidden_low, full_down)).astype(jnp.bfloat16)
    back_gate, back_up, back_down = (
        lax.all_gather(w_gate, ("seq", "ctx"), axis=0, tiled=True),
        lax.all_gather(w_up, ("seq", "ctx"), axis=0, tiled=True),
        lax.all_gather(w_down, ("seq", "ctx"), axis=0, tiled=True),
    )
    grad_hidden = product_right(upstream, back_down)
    grad_down = lax.psum_scatter(
        product_left(hidden_low, upstream), ("seq", "ctx"), scatter_dimension=0, tiled=True
    )
    grad_gate_act, grad_up_act = pull_hidden(grad_hidden)
    gate_low = grad_gate_act.astype(jnp.bfloat16)
    up_low = grad_up_act.astype(jnp.bfloat16)
    grad_normed_two = product_right(gate_low, back_gate) + product_right(up_low, back_up)
    resid_part, grad_gain_mlp = pull_two(grad_normed_two)
    grad_resid = upstream.astype(jnp.float32) + resid_part
    grad_gate, grad_up, grad_mlp_gain = (
        lax.psum_scatter(
            product_left(low_two, gate_low), ("seq", "ctx"), scatter_dimension=0, tiled=True
        ),
        lax.psum_scatter(
            product_left(low_two, up_low), ("seq", "ctx"), scatter_dimension=0, tiled=True
        ),
        lax.psum_scatter(grad_gain_mlp, ("seq", "ctx"), scatter_dimension=0, tiled=True),
    )
    back_query, back_key, back_value, back_out = (
        lax.all_gather(w_query, ("seq", "ctx"), axis=0, tiled=True),
        lax.all_gather(w_key, ("seq", "ctx"), axis=0, tiled=True),
        lax.all_gather(w_value, ("seq", "ctx"), axis=0, tiled=True),
        lax.all_gather(w_out, ("seq", "ctx"), axis=0, tiled=True),
    )
    resid_low = grad_resid.astype(jnp.bfloat16)
    grad_out_part = product_left(heads_low, resid_low)
    grad_heads = (
        product_right(resid_low, back_out)
        .astype(jnp.bfloat16)
        .reshape(rows, KV_HEADS, group, HEAD_DIM)
    )
    share_again = jnp.exp(score_block() - log_total)
    grad_share = jnp.einsum(
        "tkgd,skd->kgts", grad_heads, values_three, preferred_element_type=jnp.float32
    )
    grad_values_all = jnp.einsum(
        "kgts,tkgd->skd",
        share_again.astype(jnp.bfloat16),
        grad_heads,
        preferred_element_type=jnp.float32,
    )
    balance = jnp.sum(share_again * grad_share, axis=-1, keepdims=True)
    grad_scores = (share_again * (grad_share - balance)).astype(jnp.bfloat16)
    grad_query_rot = (
        jnp.einsum("kgts,skd->tkgd", grad_scores, keys_three, preferred_element_type=jnp.float32)
        * scale
    )
    grad_keys_all = (
        jnp.einsum("kgts,tkgd->skd", grad_scores, query_low, preferred_element_type=jnp.float32)
        * scale
    )
    grad_keys, grad_values = (
        lax.psum_scatter(
            grad_keys_all.reshape(length, KV_HEADS * HEAD_DIM),
            "ctx",
            scatter_dimension=0,
            tiled=True,
        ),
        lax.psum_scatter(
            grad_values_all.reshape(length, KV_HEADS * HEAD_DIM),
            "ctx",
            scatter_dimension=0,
            tiled=True,
        ),
    )
    grad_query_raw, grad_gain_query = pull_query(grad_query_rot.reshape(rows, HEADS, HEAD_DIM))
    grad_key_raw, grad_gain_key = pull_key(grad_keys.reshape(rows, KV_HEADS, HEAD_DIM))
    query_back = grad_query_raw.reshape(rows, HEADS * HEAD_DIM).astype(jnp.bfloat16)
    key_back = grad_key_raw.reshape(rows, KV_HEADS * HEAD_DIM).astype(jnp.bfloat16)
    value_back = grad_values.astype(jnp.bfloat16)
    grad_normed_one = (
        product_right(query_back, back_query)
        + product_right(key_back, back_key)
        + product_right(value_back, back_value)
    )
    input_part, grad_gain_attn = pull_one(grad_normed_one)
    grad_tokens = grad_resid + input_part
    grad_query, grad_key, grad_value, grad_out, grad_attn_gain, grad_query_gain, grad_key_gain = (
        lax.psum_scatter(
            product_left(low_one, query_back), ("seq", "ctx"), scatter_dimension=0, tiled=True
        ),
        lax.psum_scatter(
            product_left(low_one, key_back), ("seq", "ctx"), scatter_dimension=0, tiled=True
        ),
        lax.psum_scatter(
            product_left(low_one, value_back), ("seq", "ctx"), scatter_dimension=0, tiled=True
        ),
        lax.psum_scatter(grad_out_part, ("seq", "ctx"), scatter_dimension=0, tiled=True),
        lax.psum_scatter(grad_gain_attn, ("seq", "ctx"), scatter_dimension=0, tiled=True),
        lax.psum_scatter(grad_gain_query, ("seq", "ctx"), scatter_dimension=0, tiled=True),
        lax.psum_scatter(grad_gain_key, ("seq", "ctx"), scatter_dimension=0, tiled=True),
    )
    return (
        block_out[None],
        grad_tokens[None],
        grad_query,
        grad_key,
        grad_value,
        grad_out,
        grad_gate,
        grad_up,
        grad_down,
        grad_attn_gain,
        grad_mlp_gain,
        grad_query_gain,
        grad_key_gain,
    )


def head_order(parts):
    half = parts // 2
    return [2 * (c % half) + c // half for c in range(parts)]


PAD = 16
DIGIT = 128


def fold_qkv_kernel(parts, query, key, value, gains, positions, out):
    own = query.shape[0]
    group = query.shape[1] // parts
    head = key.shape[1] // parts
    where = positions[...]
    high = (where >> 7).astype(jnp.float32).astype(jnp.bfloat16)
    rest = (where & (DIGIT - 1)).astype(jnp.float32).astype(jnp.bfloat16)
    rows = where.shape[1]
    count = gains.shape[1]
    for c, k in enumerate(head_order(parts)):
        out[c, :own, :group] = query[:, k * group : (k + 1) * group]
        out[c, :own, group : group + head] = key[:, k * head : (k + 1) * head]
        out[c, :own, group + head :] = value[:, k * head : (k + 1) * head]
        out[c, own:, :] = jnp.zeros((PAD, out.shape[2]), out.dtype)
        out[c, own : own + 1, :count] = gains[...]
        out[c, own + 1 : own + 2, :rows] = high
        out[c, own + 1 : own + 2, rows : 2 * rows] = rest


def fold_qkv(w_query, w_key, w_value, gains, positions, parts):
    own = w_query.shape[0]
    cols = (w_query.shape[1] + w_key.shape[1] + w_value.shape[1]) // parts
    return pl.pallas_call(
        partial(fold_qkv_kernel, parts),
        out_shape=jax.ShapeDtypeStruct((parts, own + PAD, cols), w_query.dtype),
        cost_estimate=pl.CostEstimate(flops=0, bytes_accessed=1200000, transcendentals=0),
    )(w_query, w_key, w_value, gains, positions)


def fold_ff_kernel(seqs, parts, gate, up, out):
    unit = gate.shape[1] // (seqs * parts)
    for c in range(parts):
        for s in range(seqs):
            at = (s * parts + c) * unit
            out[c, :, s * unit : (s + 1) * unit] = gate[:, at : at + unit]
            out[c, :, (seqs + s) * unit : (seqs + s + 1) * unit] = up[:, at : at + unit]


def fold_ff(w_gate, w_up, seqs, parts):
    own, hidden = w_gate.shape
    return pl.pallas_call(
        partial(fold_ff_kernel, seqs, parts),
        out_shape=jax.ShapeDtypeStruct((parts, own, 2 * hidden // parts), w_gate.dtype),
        cost_estimate=pl.CostEstimate(flops=0, bytes_accessed=3200000, transcendentals=0),
    )(w_gate, w_up)


def unfold_ff_kernel(seqs, parts, turned, gate, up):
    unit = gate.shape[1] // (seqs * parts)
    for c in range(parts):
        for s in range(seqs):
            at = (s * parts + c) * unit
            gate[:, at : at + unit] = turned[c, :, s * unit : (s + 1) * unit].astype(gate.dtype)
            up[:, at : at + unit] = turned[
                c, :, (seqs + s) * unit : (seqs + s + 1) * unit
            ].astype(up.dtype)


def unfold_ff(turned, seqs, parts):
    own = turned.shape[1]
    shape = jax.ShapeDtypeStruct((own, turned.shape[2] * parts // 2), jnp.float32)
    return pl.pallas_call(
        partial(unfold_ff_kernel, seqs, parts),
        out_shape=(shape, shape),
        cost_estimate=pl.CostEstimate(flops=0, bytes_accessed=5000000, transcendentals=0),
    )(turned)


def unfold_qkv_kernel(turned, query, key, value, gains):
    parts = turned.shape[0]
    own = query.shape[0]
    group = query.shape[1] // parts
    head = key.shape[1] // parts
    total = jnp.zeros((1, turned.shape[2]), jnp.float32)
    for c, k in enumerate(head_order(parts)):
        query[:, k * group : (k + 1) * group] = turned[c, :own, :group].astype(jnp.float32)
        key[:, k * head : (k + 1) * head] = turned[c, :own, group : group + head].astype(
            jnp.float32
        )
        value[:, k * head : (k + 1) * head] = turned[c, :own, group + head :].astype(jnp.float32)
        total = total + turned[c, own:, :].astype(jnp.float32)[:1]
    gains[...] = total


def unfold_qkv(turned, own):
    parts, _, cols = turned.shape
    group = cols * HEADS // (HEADS + 2 * KV_HEADS)
    head = (cols - group) // 2
    return pl.pallas_call(
        unfold_qkv_kernel,
        out_shape=(
            jax.ShapeDtypeStruct((own, parts * group), jnp.float32),
            jax.ShapeDtypeStruct((own, parts * head), jnp.float32),
            jax.ShapeDtypeStruct((own, parts * head), jnp.float32),
            jax.ShapeDtypeStruct((1, cols), jnp.float32),
        ),
        cost_estimate=pl.CostEstimate(flops=0, bytes_accessed=1900000, transcendentals=0),
    )(turned)


ROWS = 256


def turn_halves(value):
    return pltpu.roll(value, value.shape[1] // 2, 1)


def dot_right(left, right):
    return lax.dot_general(
        left, right, (((1,), (1,)), ((), ())), preferred_element_type=jnp.float32
    )


def dot_left(left, right):
    return lax.dot_general(
        left, right, (((0,), (0,)), ((), ())), preferred_element_type=jnp.float32
    )


def project_kernel(
    own, tokens, gathered, gain, cosine, sine, gain_query, gain_key,
    normed, raw, query, key, value, weight,
):
    head = gain_query.shape[1]
    group = query.shape[1] // head

    @pl.when(pl.program_id(0) == 0)
    def _():
        weight[...] = gathered[:, :own, :].reshape(weight.shape)

    x = tokens[...].astype(jnp.float32)
    low = root_norm(x, gain[...]).astype(jnp.bfloat16)
    normed[...] = low
    qkv = jnp.dot(low, weight[...], preferred_element_type=jnp.float32)
    raw[...] = qkv[:, : (group + 1) * head]
    value[...] = qkv[:, (group + 1) * head :].astype(jnp.bfloat16)
    cos = cosine[...]
    sin = sine[...]
    for h in range(group + 1):
        scale = gain_key[...] if h == group else gain_query[...]
        part = root_norm(qkv[:, h * head : (h + 1) * head], scale)
        part = (part * cos + turn_halves(part) * sin).astype(jnp.bfloat16)
        if h == group:
            key[...] = part
        else:
            query[:, h * head : (h + 1) * head] = part


def project(tokens, gathered, gain, cosine, sine, gain_query, gain_key, own):
    length, width = tokens.shape
    cols = gathered.shape[2]
    head = gain_query.shape[1]
    rows = min(ROWS, length)

    def block(n):
        return pl.BlockSpec((rows, n), lambda i: (i, 0))

    def whole(*shape):
        return pl.BlockSpec(shape, lambda i: (0,) * len(shape))

    def out(n, kind=jnp.bfloat16):
        return jax.ShapeDtypeStruct((length, n), kind)

    raw_cols = cols - head
    return pl.pallas_call(
        partial(project_kernel, own),
        grid=(length // rows,),
        in_specs=[
            block(width),
            whole(*gathered.shape),
            whole(1, width),
            block(head),
            block(head),
            whole(1, head),
            whole(1, head),
        ],
        out_specs=[
            block(width),
            block(raw_cols),
            block(raw_cols - head),
            block(head),
            block(head),
            whole(width, cols),
        ],
        out_shape=[
            out(width),
            out(raw_cols, jnp.float32),
            out(raw_cols - head),
            out(head),
            out(head),
            jax.ShapeDtypeStruct((width, cols), jnp.bfloat16),
        ],
        cost_estimate=pl.CostEstimate(
            flops=2 * length * width * cols, bytes_accessed=14000000, transcendentals=0
        ),
        compiler_params=pltpu.CompilerParams(vmem_limit_bytes=24 * 2**20),
    )(tokens, gathered, gain, cosine, sine, gain_query, gain_key)


def block_mask(start, first, rows, keys):
    spot = first + lax.broadcasted_iota(jnp.int32, (rows, keys), 0)
    other = lax.broadcasted_iota(jnp.int32, (rows, keys), 1)
    return (other <= spot) & (other >= start)


def attend_kernel(query, key, value, start, heads, lse):
    length = query.shape[0]
    head = key.shape[1]
    rows = min(ROWS, length)
    scale = head ** (-0.5)
    for i in range(length // rows):
        at = slice(i * rows, (i + 1) * rows)
        keys = (i + 1) * rows
        visible = block_mask(start[at, :], i * rows, rows, keys)
        for h in range(query.shape[1] // head):
            of = slice(h * head, (h + 1) * head)
            scores = dot_right(query[at, of], key[:keys, :]) * scale
            scores = jnp.where(visible, scores, NEG)
            peak = jnp.max(scores, axis=1, keepdims=True)
            powers = jnp.exp(scores - peak)
            total = jnp.sum(powers, axis=1, keepdims=True)
            share = (powers / total).astype(jnp.bfloat16)
            heads[at, of] = jnp.dot(
                share, value[:keys, :], preferred_element_type=jnp.float32
            ).astype(jnp.bfloat16)
            lse[at, h : h + 1] = peak + jnp.log(total)


def attend(query, key, value, start):
    length, cols = query.shape
    return pl.pallas_call(
        attend_kernel,
        out_shape=(
            jax.ShapeDtypeStruct((length, cols), jnp.bfloat16),
            jax.ShapeDtypeStruct((length, cols // key.shape[1]), jnp.float32),
        ),
        cost_estimate=pl.CostEstimate(
            flops=4 * length * length * cols, bytes_accessed=2600000, transcendentals=2 * length * length
        ),
        compiler_params=pltpu.CompilerParams(vmem_limit_bytes=24 * 2**20),
    )(query, key, value, start)


def norm_back(raw, gain, grad):
    r = lax.rsqrt(jnp.mean(raw * raw, axis=1, keepdims=True) + EPS)
    weighted = gain * grad
    back = r * weighted - (r * r * r) * raw * jnp.mean(weighted * raw, axis=1, keepdims=True)
    return back, jnp.sum(grad * raw * r, axis=0, keepdims=True)


def attend_back_kernel(
    query, key, value, start, lse, grads, raw, cosine, sine, gain_query, gain_key,
    back, part_query, part_key, grad_key, grad_value,
):
    length = query.shape[0]
    head = key.shape[1]
    group = query.shape[1] // head
    rows = min(ROWS, length)
    scale = head ** (-0.5)
    low = jnp.bfloat16
    grad_key[...] = jnp.zeros_like(grad_key)
    grad_value[...] = jnp.zeros_like(grad_value)
    total_query = jnp.zeros((1, head), jnp.float32)
    total_key = jnp.zeros((1, head), jnp.float32)
    for i in range(length // rows):
        at = slice(i * rows, (i + 1) * rows)
        keys = (i + 1) * rows
        visible = block_mask(start[at, :], i * rows, rows, keys)
        cos = cosine[at, :]
        sin = sine[at, :]
        for h in range(group):
            of = slice(h * head, (h + 1) * head)
            one = query[at, of]
            grad = grads[at, of]
            scores = jnp.where(visible, dot_right(one, key[:keys, :]) * scale, NEG)
            share = jnp.exp(scores - lse[at, h : h + 1])
            grad_share = dot_right(grad, value[:keys, :])
            grad_value[:keys, :] += dot_left(share.astype(low), grad)
            balance = jnp.sum(share * grad_share, axis=1, keepdims=True)
            grad_scores = (share * (grad_share - balance)).astype(low)
            turned = (
                jnp.dot(grad_scores, key[:keys, :], preferred_element_type=jnp.float32) * scale
            )
            grad_key[:keys, :] += dot_left(grad_scores, one)
            turned = turned * cos - turn_halves(turned) * sin
            result, term = norm_back(raw[at, of], gain_query[...], turned)
            back[at, of] = result.astype(low)
            total_query += term
    of = slice(group * head, (group + 1) * head)
    for i in range(length // rows):
        at = slice(i * rows, (i + 1) * rows)
        turned = grad_key[at, :] * scale
        turned = turned * cosine[at, :] - turn_halves(turned) * sine[at, :]
        result, term = norm_back(raw[at, of], gain_key[...], turned)
        back[at, of] = result.astype(low)
        total_key += term
        back[at, (group + 1) * head :] = grad_value[at, :].astype(low)
    part_query[...] = total_query
    part_key[...] = total_key


def attend_back(query, key, value, start, lse, grads, raw, cosine, sine, gain_query, gain_key):
    length, cols = query.shape
    head = key.shape[1]
    row = jax.ShapeDtypeStruct((1, head), jnp.float32)
    return pl.pallas_call(
        attend_back_kernel,
        out_shape=(
            jax.ShapeDtypeStruct((length, cols + 2 * head), jnp.bfloat16),
            row,
            row,
        ),
        scratch_shapes=[
            pltpu.VMEM((length, head), jnp.float32),
            pltpu.VMEM((length, head), jnp.float32),
        ],
        cost_estimate=pl.CostEstimate(
            flops=10 * length * length * cols, bytes_accessed=6000000, transcendentals=2 * length * length
        ),
        compiler_params=pltpu.CompilerParams(vmem_limit_bytes=28 * 2**20),
    )(query, key, value, start, lse, grads, raw, cosine, sine, gain_query, gain_key)


def pack_grads_kernel(own, normed, back, attn, mlp, query, key, out):
    owners = out.shape[0]
    small = query.shape[1] // owners
    low = out.dtype
    cols = out.shape[2]
    chunk = min(owners, 4)
    for first in range(0, owners, chunk):
        part = dot_left(normed[:, first * own : (first + chunk) * own], back[...]).astype(low)
        out[first : first + chunk, :own, :] = part.reshape(chunk, own, cols)
    out[:, own:, :] = jnp.zeros((owners, PAD, cols), low)
    for o in range(owners):
        row = slice(own, own + 1)
        out[o, row, :own] = attn[:, o * own : (o + 1) * own].astype(low)
        out[o, row, own : 2 * own] = mlp[:, o * own : (o + 1) * own].astype(low)
        out[o, row, 2 * own : 2 * own + small] = query[:, o * small : (o + 1) * small].astype(low)
        out[o, row, 2 * own + small : 2 * (own + small)] = key[
            :, o * small : (o + 1) * small
        ].astype(low)


def pack_grads(normed, back, attn, mlp, query, key, own):
    length, width = normed.shape
    cols = back.shape[1]
    owners = width // own
    return pl.pallas_call(
        partial(pack_grads_kernel, own),
        out_shape=jax.ShapeDtypeStruct((owners, own + PAD, cols), jnp.bfloat16),
        cost_estimate=pl.CostEstimate(
            flops=2 * length * width * cols, bytes_accessed=8000000, transcendentals=0
        ),
        compiler_params=pltpu.CompilerParams(vmem_limit_bytes=24 * 2**20),
    )(normed, back, attn, mlp, query, key).reshape(-1, cols)


def feed_kernel(count, *refs):
    arrived = refs[:count]
    upstream = refs[count : 2 * count]
    w_gu, w_down, hidden_out, gate_out, up_out, part_out, part_two = refs[2 * count :]
    low = jnp.bfloat16
    wide = w_down.shape[0]

    def join(pieces):
        return jnp.concatenate([piece[...] for piece in pieces], axis=0)

    normed = join(arrived)
    gate = jnp.dot(normed, w_gu[:, :wide], preferred_element_type=jnp.float32)
    up = jnp.dot(normed, w_gu[:, wide:], preferred_element_type=jnp.float32)
    grad_hidden = dot_right(join(upstream), w_down[...])
    s = jax.nn.sigmoid(gate)
    silu = gate * s
    hidden = (silu * up).astype(low)
    grad_gate = (grad_hidden * up * s * (1.0 + gate * (1.0 - s))).astype(low)
    grad_up = (grad_hidden * silu).astype(low)
    hidden_out[...] = hidden
    gate_out[...] = grad_gate
    up_out[...] = grad_up
    part_out[...] = jnp.dot(hidden, w_down[...], preferred_element_type=jnp.float32).astype(low)
    part_two[...] = (
        dot_right(grad_gate, w_gu[:, :wide]) + dot_right(grad_up, w_gu[:, wide:])
    ).astype(low)


def feed(arrived, upstream, w_gu, w_down):
    count = len(arrived)
    wide, width = w_down.shape
    rows = sum(item.shape[0] for item in arrived)
    low = jnp.bfloat16
    return pl.pallas_call(
        partial(feed_kernel, count),
        out_shape=[jax.ShapeDtypeStruct((rows, wide), low)] * 3
        + [jax.ShapeDtypeStruct((rows, width), low)] * 2,
        cost_estimate=pl.CostEstimate(
            flops=12 * rows * width * wide,
            bytes_accessed=6 * width * wide + 12 * rows * width,
            transcendentals=rows * wide,
        ),
        compiler_params=pltpu.CompilerParams(vmem_limit_bytes=22 * 2**20),
    )(*arrived, *upstream, w_gu, w_down)


def outer_kernel(counts, rights, *refs):
    out = refs[-1]
    at = 0
    lefts = []
    for count in counts:
        lefts.append(jnp.concatenate([item[...] for item in refs[at : at + count]], axis=0))
        at += count
    first = 0
    for sizes in rights:
        total = None
        for left, size in zip(lefts, sizes):
            right = jnp.concatenate([item[...] for item in refs[at : at + size]], axis=0)
            at += size
            term = dot_left(left, right)
            total = term if total is None else total + term
        out[:, first : first + total.shape[1]] = total.astype(out.dtype)
        first += total.shape[1]


def outer_sum(lefts, rights, tile):
    flat_left = [item for group in lefts for item in group]
    flat_right = [item for side in rights for group in side for item in group]
    tall = flat_left[0].shape[1]
    cols = sum(side[0][0].shape[1] for side in rights)
    length = sum(item.shape[0] for item in flat_left)
    return pl.pallas_call(
        partial(
            outer_kernel,
            [len(group) for group in lefts],
            [[len(group) for group in side] for side in rights],
        ),
        grid=(tall // tile,),
        in_specs=[pl.BlockSpec((item.shape[0], tile), lambda i: (0, i)) for item in flat_left]
        + [pl.BlockSpec(item.shape, lambda i: (0, 0)) for item in flat_right],
        out_specs=pl.BlockSpec((tile, cols), lambda i: (i, 0)),
        out_shape=jax.ShapeDtypeStruct((tall, cols), jnp.bfloat16),
        cost_estimate=pl.CostEstimate(
            flops=2 * tall * cols * length,
            bytes_accessed=2 * (tall * cols + length * (tall + cols)),
            transcendentals=0,
        ),
        compiler_params=pltpu.CompilerParams(vmem_limit_bytes=18 * 2**20),
    )(*flat_left, *flat_right)


def angles(where, head):
    half = head // 2
    freq = THETA ** (-jnp.arange(half, dtype=jnp.float32) * 2.0 / head)
    angle = where.astype(jnp.float32)[:, None] * freq[None, :]
    cosine = jnp.cos(angle)
    sine = jnp.sin(angle)
    return jnp.concatenate([cosine, cosine], axis=-1), jnp.concatenate([-sine, sine], axis=-1)


def grouped_body(
    seqs,
    parts,
    tokens,
    positions,
    cotangent,
    w_query,
    w_key,
    w_value,
    w_out,
    w_gate,
    w_up,
    w_down,
    attn_gain,
    mlp_gain,
    query_gain,
    key_gain,
):
    rows = tokens.shape[1]
    own = w_query.shape[0]
    group = HEADS // KV_HEADS
    length = rows * parts
    low = jnp.bfloat16
    unit = w_gate.shape[1] // (seqs * parts)
    wide = seqs * unit
    reach = parts // 2
    part = lax.axis_index("ctx")
    here = lax.axis_index("seq")
    small = query_gain.shape[0]

    ring = list(range(0, parts, 2)) + list(range(parts - 1, 0, -2))
    onward = [(ring[k], ring[(k + 1) % parts]) for k in range(parts)]
    backward = [(b, a) for a, b in onward]

    def right(value):
        return lax.ppermute(value, "ctx", onward)

    def left(value):
        return lax.ppermute(value, "ctx", backward)

    spot = jnp.where(part & 1 == 0, part >> 1, parts - ((part + 1) >> 1))
    begin = {}
    for step in range(1 - reach, reach + 1):
        ahead = (spot + (parts + step)) & (parts - 1)
        begin[step] = jnp.where(ahead < reach, 2 * ahead, 2 * (parts - ahead) - 1) * rows

    def hold(values, others):
        return lax.optimization_barrier((values, others))[0]

    done = {}

    def step_out(sent, jobs):
        sent = hold(sent, ())
        got = [(right(ahead), left(behind)) for ahead, behind in sent]
        job = jobs.pop(0) if jobs else None
        got, made = hold((got, () if job is None else job(sent)), ())
        if isinstance(made, dict):
            done.update(made)
        return got

    def ring_pieces(value, jobs=()):
        jobs = list(jobs)
        half = rows // 2
        pieces = [(value,)]
        ahead = behind = value
        for step in range(1, reach + 1):
            if step == reach:
                ahead, behind = ahead[:half], behind[half:]
            if jobs and jobs[0] is not None:
                jobs[0] = partial(jobs[0], pieces[-1])
            ((ahead, behind),) = step_out([(ahead, behind)], jobs)
            pieces.append((ahead, behind))
        return pieces

    def ring_gather(value, base, jobs=()):
        def drop(job):
            return None if job is None else lambda piece, sent: job(sent)

        pieces = ring_pieces(value, [drop(job) for job in jobs])
        done["last"] = pieces[-1]
        return whole_of(pieces, base)

    def whole_of(pieces, base):
        put = partial(lax.dynamic_update_slice_in_dim, axis=0, allow_negative_indices=False)
        whole = put(base, pieces[0][0], begin[0])
        for step in range(1, reach):
            whole = put(put(whole, pieces[step][0], begin[-step]), pieces[step][1], begin[step])
        whole = put(whole, pieces[reach][0], begin[reach])
        return put(whole, pieces[reach][1], begin[reach] + rows // 2)

    def ring_scatter(rings, jobs=()):
        jobs = list(jobs)
        half = rows // 2
        wider = jnp.float32

        def widen(pair):
            return pair[0].astype(wider), pair[1].astype(wider)

        got = step_out([(terms[reach][:half], terms[reach][half:]) for terms in rings], jobs)
        got = [
            (jnp.pad(ahead, ((0, half), (0, 0))), jnp.pad(behind, ((half, 0), (0, 0))))
            for ahead, behind in map(widen, got)
        ]
        for step in range(reach - 1, 0, -1):
            sent = [
                (
                    (terms[step][rows:].astype(wider) + ahead).astype(low),
                    (terms[step][:rows].astype(wider) + behind).astype(low),
                )
                for terms, (ahead, behind) in zip(rings, got)
            ]
            got = [widen(pair) for pair in step_out(sent, jobs)]
        return [
            terms[0].astype(wider) + ahead + behind for terms, (ahead, behind) in zip(rings, got)
        ]

    def ring_terms(value):
        def cut(step):
            return lax.dynamic_slice_in_dim(
                value, begin[step], rows, 0, allow_negative_indices=False
            ).astype(low)

        pairs = [jnp.concatenate([cut(-step), cut(step)]) for step in range(1, reach)]
        return [cut(0)] + pairs + [cut(reach)]

    def seq_gather(value):
        return lax.all_gather(value, "seq", axis=0, tiled=True)

    def seq_scatter(value):
        return lax.psum_scatter(value.astype(low), "seq", scatter_dimension=0, tiled=True)

    def cross(value, bit):
        return lax.ppermute(value, "seq", [(s, s ^ bit) for s in range(seqs)])

    def seq_scatter_near(value):
        size = value.shape[0] // seqs

        def cut(bits):
            return lax.dynamic_slice_in_dim(
                value, (here ^ bits) * size, size, 0, allow_negative_indices=False
            ).astype(low)

        far = cross(cut(3), 1).astype(jnp.float32)
        near = cross(cut(1), 1).astype(jnp.float32)
        other = cross((cut(2) + far).astype(low), 2).astype(jnp.float32)
        return cut(0) + near + other

    def turn(value):
        return lax.all_to_all(value, "ctx", split_axis=0, concat_axis=0, tiled=True)

    def swap_rows(value, back=False):
        pairs = [
            (a, (a % seqs) * parts + head_order(parts).index(a // seqs))
            for a in range(seqs * parts)
        ]
        if back:
            pairs = [(b, a) for a, b in pairs]
        return lax.ppermute(value, ("seq", "ctx"), pairs)

    my_x = tokens[0].astype(jnp.float32)
    upstream = cotangent[0]
    wide_q = group * HEAD_DIM
    wide_qkv = wide_q + 2 * HEAD_DIM
    tall = own + PAD
    packed = fold_qkv(
        w_query,
        w_key,
        w_value,
        jnp.concatenate([attn_gain, mlp_gain, query_gain, key_gain])[None],
        positions,
        parts,
    )

    def pack_first(sent):
        return packed

    def pack_second(sent):
        done["turned"] = turn(hold(packed, sent))
        done["folded"] = fold_ff(*hold((w_gate, w_up), sent), seqs, parts)
        return done["folded"]

    def pack_third(sent):
        done["turned"] = hold(done["turned"], sent)
        return ()

    def angle_part(sent):
        digits = done["turned"][:, own + 1, : 2 * rows].astype(jnp.float32)
        where = digits[:, :rows] * DIGIT + digits[:, rows:]
        done["where"] = hold(where.astype(jnp.int32).reshape(-1), sent)
        done["angles"] = angles(done["where"], HEAD_DIM)
        return done["angles"]

    full_x = ring_gather(
        tokens[0],
        jnp.zeros((length, tokens.shape[2]), low),
        [pack_first, pack_second, pack_third, angle_part],
    )
    turned = done["turned"]
    gathered = seq_gather(turned.reshape(parts * tall, wide_qkv)).reshape(-1, tall, wide_qkv)
    gains = gathered[:, own, : 2 * (own + small)].astype(jnp.float32)
    gain_attn = gains[:, :own].reshape(-1)
    gain_mlp = gains[:, own : 2 * own].reshape(-1)
    gain_query = gains[:, 2 * own : 2 * own + small].reshape(1, -1)
    gain_key = gains[:, 2 * own + small :].reshape(1, -1)
    start = (jnp.arange(length, dtype=jnp.int32) - done["where"])[:, None]
    cosine, sine = done["angles"]

    turned_gu = turn(hold(done["folded"], done["last"])).reshape(own * parts, -1)
    w_d = seq_gather(w_down)

    def first_part(sent):
        full, _ = hold((full_x, gathered), sent)
        done["first"] = project(
            full, gathered, gain_attn[None], cosine, sine, gain_query, gain_key, own
        )
        done["swapped"] = swap_rows(hold(w_out, sent))
        return done["first"], done["swapped"]

    def second_part(sent):
        _, _, query, key, value, _ = hold(done["first"], sent)
        done["w_out"] = seq_gather(hold(done["swapped"], sent))
        done["second"] = attend(query, key, value, start)
        return done["second"]

    def drop(job):
        return lambda piece, sent: job(sent)

    pieces_c = ring_pieces(hold(upstream, done["last"]), [drop(first_part), drop(second_part)])
    low_one, raw, query_low, key_low, value_low, w_qkv = done["first"]
    heads_low, lse = done["second"]
    w_o = done["w_out"]
    turned_gu, heads_low = hold((turned_gu, heads_low), (pieces_c[reach], w_d))
    w_gu = seq_gather(turned_gu)
    (summed,) = ring_scatter([ring_terms(product(hold(heads_low, turned_gu), w_o))])
    resid = my_x + summed

    normed_two, pull_two = jax.vjp(root_norm, resid, gain_mlp)
    fed = []

    def feed_next(piece, sent=()):
        fed.append(feed(hold(piece, sent), pieces_c[len(fed)], w_gu, w_d))
        return fed[-1]

    pieces_two = ring_pieces(normed_two.astype(low), [feed_next] * reach)
    feed_next(pieces_two[reach])
    hidden, grad_gate_act, grad_up_act, part_out, part_two = zip(*fed)

    def singly(items):
        return [(item,) for item in items]

    def sum_gu(sent):
        return {
            "gu": outer_sum(
                hold(pieces_two, sent), [singly(grad_gate_act), singly(grad_up_act)], 512
            )
        }

    def sum_down(sent):
        done["down"] = outer_sum(singly(hold(hidden, sent)), [pieces_c], 384)
        return done["down"]

    grad_normed_two, summed = ring_scatter([part_two, part_out], [sum_down, sum_gu])
    done["gu"] = seq_scatter(done["gu"])
    resid_part, part_mlp = pull_two(grad_normed_two)
    block_out = (resid + summed).astype(low)
    grad_resid = upstream.astype(jnp.float32) + resid_part
    heads_back = []

    def back_heads(piece, sent):
        heads_back.append(
            [product_right(item, w_o).astype(low) for item in hold(piece, sent)]
        )
        return heads_back[-1]

    def spread_down(piece, sent):
        done["down"] = seq_scatter_near(hold(done["down"], sent))
        return back_heads(piece, sent)

    def end_down(piece, sent):
        done["sent"] = sent
        return back_heads(piece, sent), done["down"]

    pieces_resid = ring_pieces(
        grad_resid.astype(low), [spread_down, back_heads, back_heads, end_down]
    )
    turned_grad = turn(hold(done["gu"], done["sent"]).reshape(parts, own, 2 * wide))
    back_heads(pieces_resid[reach], ())
    grad_heads = whole_of(heads_back, jnp.zeros((length, wide_q), low))
    done["back"] = attend_back(
        query_low,
        key_low,
        value_low,
        start,
        lse,
        grad_heads,
        raw,
        cosine,
        sine,
        gain_query,
        gain_key,
    )
    qkv_back, part_query, part_key = done["back"]
    part_normed_one = product_right(qkv_back, w_qkv)
    _, pull_gain = jax.vjp(
        lambda gain: root_norm(full_x.astype(jnp.float32), gain), gain_attn
    )

    def sum_qkv(sent):
        held = hold(qkv_back, sent)
        done["qkv"] = pack_grads(
            low_one,
            held,
            pull_gain(part_normed_one)[0][None],
            part_mlp[None],
            part_query,
            part_key,
            own,
        )
        pieces = [
            [lax.dynamic_slice_in_dim(heads_low, begin[0], rows, 0, allow_negative_indices=False)]
        ]
        half = rows // 2
        for step in range(1, reach + 1):
            size = rows if step < reach else half
            pieces.append(
                [
                    lax.dynamic_slice_in_dim(
                        heads_low, at, size, 0, allow_negative_indices=False
                    )
                    for at in (
                        (begin[-step], begin[step])
                        if step < reach
                        else (begin[reach], begin[reach] + half)
                    )
                ]
            )
        done["out"] = outer_sum(pieces, [hold(pieces_resid, sent)], wide_q)
        done["turned"] = hold(turned_grad, sent)
        return done["qkv"], done["out"], done["turned"]

    def end_gu(sent):
        done["gu"] = unfold_ff(hold(done["turned"], sent), seqs, parts)
        return done["gu"]

    (grad_normed_one,) = ring_scatter([ring_terms(part_normed_one)], [sum_qkv, end_gu])
    grad_gate, grad_up = done["gu"]
    grad_down = done["down"]
    summed = seq_scatter_near(done["qkv"]).astype(low)
    grad_query, grad_key, grad_value, gain_sums = unfold_qkv(
        turn(summed.reshape(parts, tall, wide_qkv)), own
    )
    gain_sums = gain_sums[0]
    grad_out = swap_rows(seq_scatter(done["out"]), back=True).astype(jnp.float32)
    _, pull_mine = jax.vjp(lambda value: root_norm(value, gain_attn), my_x)
    grad_tokens = grad_resid + pull_mine(grad_normed_one)[0]
    return (
        block_out[None],
        grad_tokens[None],
        grad_query,
        grad_key,
        grad_value,
        grad_out,
        grad_gate,
        grad_up,
        grad_down,
        gain_sums[:own],
        gain_sums[own : 2 * own],
        gain_sums[2 * own : 2 * own + small],
        gain_sums[2 * own + small : 2 * (own + small)],
    )


def solution(mesh):
    grouped = mesh.shape["ctx"] == KV_HEADS and mesh.shape["seq"] == 4
    return jax.shard_map(
        partial(grouped_body, mesh.shape["seq"], mesh.shape["ctx"]) if grouped else whole_body,
        mesh=mesh,
        in_specs=(
            P("seq", "ctx", None),
            P("seq", "ctx"),
            P("seq", "ctx", None),
            P(("seq", "ctx"), None),
            P(("seq", "ctx"), None),
            P(("seq", "ctx"), None),
            P(("seq", "ctx"), None),
            P(("seq", "ctx"), None),
            P(("seq", "ctx"), None),
            P(("seq", "ctx"), None),
            P(("seq", "ctx")),
            P(("seq", "ctx")),
            P(("seq", "ctx")),
            P(("seq", "ctx")),
        ),
        out_specs=(
            P("seq", "ctx", None),
            P("seq", "ctx", None),
            P(("seq", "ctx"), None),
            P(("seq", "ctx"), None),
            P(("seq", "ctx"), None),
            P(("seq", "ctx"), None),
            P(("seq", "ctx"), None),
            P(("seq", "ctx"), None),
            P(("seq", "ctx"), None),
            P(("seq", "ctx")),
            P(("seq", "ctx")),
            P(("seq", "ctx")),
            P(("seq", "ctx")),
        ),
        check_vma=False,
    )
```
